512 devices in a mesh: gx: 64 (over z, x, core), gy: 8 (over y).
Axes of the slice: x: 4, y: 8, z: 8, core: 2. Of those that a mesh axis runs over, the one named last changes fastest.
Arguments:
- pressure_source: float32 [512, 256, 256], P('gx', 'gy'), may hold values from -120 to 120
- conductance: float32 [512, 256, 256], P('gx', 'gy'), may hold values from 1 to 10
Outputs:
- pressure: float32 [512, 256, 256], P('gx', 'gy')
- residual: float32 [512, 256, 256], P('gx', 'gy')
The draws below stay inside these ranges and needn't reach their ends.
All inputs are finite; a program needn't handle non-finite values.
Results may differ from the reference program's by a relative error of at most 0.0003.
Values sent between devices are 32-bit elements; how exact they have to be, the bound alone decides.
No kernel may reach another device: no remote copies, remote signals or barrier semaphores. Data moves between devices by JAX's collectives and lax.ppermute only.
A program may use at most 64 MiB of HBM per device.

```python
import math
import jax
import jax.numpy as jnp

NZ = 256
LEVELS = 3
DEGREE = 3
COARSE_DEG = 6
NX = 512
NY = 256


def level_of(rng, dims, cuts, smallest, high):
    loudness, own = 1.0, jax.random.fold_in(rng, 6)
    for axis_at, blocks in cuts:
        draws = jnp.exp(jax.random.uniform(jax.random.fold_in(own, axis_at), (blocks,), jnp.float32, smallest / len(cuts), high / len(cuts)))
        loudness = loudness * jnp.repeat(draws, dims[axis_at] // blocks).reshape([-1 if axis == axis_at else 1 for axis in range(len(dims))])
    return loudness


def noise(own_key, dims, width, limit, cuts=(), held_as=jnp.bfloat16):
    entries = width * jax.random.normal(own_key, dims, jnp.float32)
    if cuts:
        entries = entries * level_of(own_key, dims, cuts, -0.22, 0.18)
    return jnp.clip(entries, -limit, limit).astype(held_as)


def setup_inputs(seed: int = 0) -> dict:
    streams_of = jax.random.split(jax.random.key(seed), 3)
    pressure_source = noise(streams_of[0], (NX, NY, NZ), 20.0, 120.0, ((0, 64), (1, 8)), jnp.float32)
    conductance = jnp.clip(jnp.exp(math.log(10.0) - 2.3025851 * jax.random.uniform(streams_of[1], (NX, NY, NZ), jnp.float32) ** level_of(streams_of[1], (NX, NY, NZ), ((0, 64), (1, 8)), -0.2, 0.2)), 1.0, 10.0)
    return {"pressure_source": pressure_source, "conductance": conductance}


cheb_center = 1.15
cheb_spread = 0.85


def zero_pad(field):
    return jnp.pad(field, 1)


def faces_of(conduct, pad_fn):
    padded = pad_fn(conduct)
    neighbours = [padded[:-2, 1:-1, 1:-1], padded[2:, 1:-1, 1:-1], padded[1:-1, :-2, 1:-1],
                  padded[1:-1, 2:, 1:-1], padded[1:-1, 1:-1, :-2], padded[1:-1, 1:-1, 2:]]
    faces = [0.5 * (conduct + other) for other in neighbours]
    diag_sum = faces[0] + faces[1] + faces[2] + faces[3] + faces[4] + faces[5]
    return faces, diag_sum


def apply_level(field, faces, diag_sum, factor, pad_fn):
    padded = pad_fn(field)
    beside_all = faces[0] * padded[:-2, 1:-1, 1:-1] + faces[1] * padded[2:, 1:-1, 1:-1]
    beside_all = beside_all + faces[2] * padded[1:-1, :-2, 1:-1] + faces[3] * padded[1:-1, 2:, 1:-1]
    beside_all = beside_all + faces[4] * padded[1:-1, 1:-1, :-2] + faces[5] * padded[1:-1, 1:-1, 2:]
    return factor * (diag_sum * field - beside_all)


def chebyshev(start, source, operator, inverse, degree):
    ratio = cheb_center / cheb_spread
    weight_old = 1.0 / ratio
    if start is None:
        update = source * inverse / cheb_center
        field = update
    else:
        update = (source - operator(start)) * inverse / cheb_center
        field = start + update
    for sweep_index in range(degree - 1):
        weight_new = 1.0 / (2.0 * ratio - weight_old)
        direct = (source - operator(field)) * inverse
        update = weight_new * weight_old * update + (2.0 * weight_new / cheb_spread) * direct
        field = field + update
        weight_old = weight_new
    return field


def restrict(field):
    size_a, size_b, size_c = field.shape
    return field.reshape(size_a // 2, 2, size_b // 2, 2, size_c // 2, 2).mean(axis=(1, 3, 5))


def prolong(coarse):
    size_a, size_b, size_c = coarse.shape
    spread_out = jnp.broadcast_to(coarse[:, None, :, None, :, None], (size_a, 2, size_b, 2, size_c, 2))
    return spread_out.reshape(size_a * 2, size_b * 2, size_c * 2)


def vcycle(source, conduct, level):
    factor = 0.25 ** level
    faces, diag_sum = faces_of(conduct, zero_pad)
    inverse = 1.0 / (factor * diag_sum)

    def operator(field):
        return apply_level(field, faces, diag_sum, factor, zero_pad)

    if level == LEVELS:
        result = chebyshev(None, source, operator, inverse, COARSE_DEG)
        remain = source - operator(result)
        line_fix = jnp.sum(remain, axis=1, keepdims=True) / jnp.sum(factor * diag_sum, axis=1, keepdims=True)
        return result + line_fix, faces, diag_sum
    result = chebyshev(None, source, operator, inverse, DEGREE)
    remain = source - operator(result)
    coarse, unused_faces, unused_diag = vcycle(restrict(remain), restrict(conduct), level + 1)
    result = result + prolong(coarse)
    result = chebyshev(result, source, operator, inverse, DEGREE)
    return result, faces, diag_sum


def reference(pressure_source, conductance):
    result, faces, diag_sum = vcycle(pressure_source, conductance, 0)
    residual = pressure_source - apply_level(result, faces, diag_sum, 1.0, zero_pad)
    return result, residual
```

```python
import functools

import jax
import jax.numpy as jnp
from jax import lax
from jax.experimental import pallas as pl
from jax.experimental.pallas import tpu as pltpu
from jax.sharding import PartitionSpec as P

CENTER = 1.15
SPREAD = 0.85
RATIO = CENTER / SPREAD
F32 = jnp.float32
BF16 = jnp.bfloat16


def cheb_weights(degree):
    old = 1.0 / RATIO
    weights = []
    for _ in range(degree - 1):
        new = 1.0 / (2.0 * RATIO - old)
        weights.append((new * old, 2.0 * new / SPREAD))
        old = new
    return weights


def selector(rows, cols, test):
    r = lax.broadcasted_iota(jnp.int32, (rows, cols), 0)
    c = lax.broadcasted_iota(jnp.int32, (rows, cols), 1)
    return jnp.where(test(r, c), 1.0, 0.0).astype(BF16)


def pick(a, chosen):
    high = a.astype(BF16)
    rest = a - high.astype(F32)
    mid = rest.astype(BF16)
    low = (rest - mid.astype(F32)).astype(BF16)
    parts = [jnp.dot(part, chosen, preferred_element_type=F32) for part in (high, mid, low)]
    return parts[0] + (parts[1] + parts[2])


def each(lo, hi, block, body):
    whole = (hi - lo) // block

    def step(i, carry):
        p = lo + i * block
        body([p + b for b in range(block)])
        return carry

    if whole == 1:
        step(0, 0)
    else:
        lax.fori_loop(0, whole, step, 0)
    rest = list(range(lo + whole * block, hi))
    if rest:
        body(rest)


class Level:
    def __init__(self, refs, block, full_y, full_z):
        self.u, self.g, self.cx, self.cy, self.cz, self.dg, self.inv, self.d, self.w = refs
        self.block, self.full_y, self.full_z = block, full_y, full_z
        self.rows, self.lanes = self.d.shape[1:]

    def from_zero(self, k_ref, lo, hi, degree):
        rows, lanes = self.rows, self.lanes
        zeros = jnp.zeros((rows, lanes), F32)
        for ref in (self.u, self.w, k_ref):
            ref[lo - 1] = zeros
            ref[hi] = zeros
        row = lax.broadcasted_iota(jnp.int32, (rows, lanes), 0)
        lane = lax.broadcasted_iota(jnp.int32, (rows, lanes), 1)
        chain = [self.u, self.w] if degree % 2 else [self.w, self.u]
        targets = (self.cx, self.cy, self.cz, self.dg, self.inv, self.g, chain[0])

        def first(planes):
            k = [k_ref[p] for p in [planes[0] - 1] + planes + [planes[-1] + 1]]
            keep = []
            for at, p in enumerate(planes):
                back, own, up = k[at:at + 3]
                ky = pltpu.roll(own, rows - 1, 0)
                kyb = pltpu.roll(own, 1, 0)
                kz = pltpu.roll(own, lanes - 1, 1)
                kzb = pltpu.roll(own, 1, 1)
                cy = 0.5 * (own + ky)
                cz = 0.5 * (own + kz)
                if self.full_y:
                    cy = jnp.where(row == rows - 1, 0.0, cy)
                    ky = jnp.where(row == rows - 1, 0.0, ky)
                    kyb = jnp.where(row == 0, 0.0, kyb)
                if self.full_z:
                    cz = jnp.where(lane == lanes - 1, 0.0, cz)
                    kz = jnp.where(lane == lanes - 1, 0.0, kz)
                    kzb = jnp.where(lane == 0, 0.0, kzb)
                dg = 3.0 * own + 0.5 * ((back + up) + (ky + kyb) + (kz + kzb))
                inside = own > 0.0
                inv = jnp.where(inside, 1.0 / jnp.where(inside, dg, 1.0), 0.0)
                g = self.g[p] * inv
                keep.append((0.5 * (own + up), cy, cz, dg, inv, g, g * (1.0 / CENTER)))
            for p, values in zip(planes, keep):
                for ref, value in zip(targets, values):
                    ref[p] = value

        self.cx[lo - 1] = 0.5 * k_ref[lo]
        each(lo, hi, self.block, first)
        for at, (a, b) in enumerate(cheb_weights(degree)):
            old, new = chain
            self.sweep(old, new, lo, hi, a, b, old if at == 0 else self.d, at < degree - 2)
            chain = [new, old]

    def from_start(self, start, lo, hi, degree, shift):
        chain = [start, self.w]
        for at, (a, b) in enumerate([(0.0, 1.0 / CENTER)] + cheb_weights(degree)):
            lo, hi = lo + 1, hi - 1
            old, new = chain
            self.sweep(old, new, lo, hi, a, b, self.d if at else None, at < degree - 1, shift)
            chain = [new, old]
        return chain[0]

    def sweep(self, old, new, lo, hi, a, b, before, keep, shift=0):
        def body(planes):
            values = []
            for p, (v, z) in zip(planes, self.scaled(old, planes, shift)):
                step = b * z
                if before is not None:
                    step = step + a * before[p]
                values.append((step, v + step))
            for p, (step, value) in zip(planes, values):
                if keep:
                    self.d[p] = step
                new[p] = value

        each(lo, hi, self.block, body)

    def scaled(self, u_ref, planes, shift=0):
        u = [u_ref[p] for p in [planes[0] - 1] + planes + [planes[-1] + 1]]
        cx = [self.cx[p + shift] for p in [planes[0] - 1] + planes]
        results = []
        for at, p in enumerate(planes):
            q = p + shift
            back, v, up = u[at:at + 3]
            cy = self.cy[q]
            cz = self.cz[q]
            s = cx[at + 1] * up + cx[at] * back
            s = s + (cy * pltpu.roll(v, self.rows - 1, 0) + pltpu.roll(cy * v, 1, 0))
            s = s + (cz * pltpu.roll(v, self.lanes - 1, 1) + pltpu.roll(cz * v, 1, 1))
            results.append((v, (self.g[q] + s * self.inv[q]) - v))
        return results

    def remain(self, u_ref, planes, shift=0):
        return [(v, z * self.dg[p + shift]) for p, (v, z) in zip(planes, self.scaled(u_ref, planes, shift))]


def fold_rows(ref, at, count):
    return ref[at, pl.ds(0, count, stride=2), :] + ref[at, pl.ds(1, count, stride=2), :]


def spread_rows(ref, at, value):
    count = value.shape[0]
    ref[at, pl.ds(0, count, stride=2), :] = value
    ref[at, pl.ds(1, count, stride=2), :] = value


def rows_at(i, count):
    return pl.ds(pl.multiple_of(i * count, count), count)


def lay_out(g, k, first, own, second, even):
    for part, to in ((0, g), (1, k)):
        to[9:17] = own[part]

    @pl.when(even)
    def _():
        for part, to in ((0, g), (1, k)):
            to[1:9] = second[part]
            to[17:25] = first[part]

    @pl.when(jnp.logical_not(even))
    def _():
        for part, to in ((0, g), (1, k)):
            to[1:9] = first[part]
            to[17:25] = second[part]


def down0(first, own, second, u, g, cx, cy, cz, dg, inv, c_out, k, d, w, pairs):
    lay_out(g, k, first, own, second, lax.axis_index("gx") % 2 == 0)
    level = Level((u, g, cx, cy, cz, dg, inv, d, w), 4, False, True)
    level.from_zero(k, 1, 25, 3)

    def fold(planes):
        (_, r), (_, r_up) = level.remain(u, planes)
        both = (r + r_up)[8:40]
        k_both = (k[planes[0]] + k[planes[1]])[8:40]
        at = rows_at((planes[0] - 1) // 2, 32)
        for half in range(2):
            lanes = slice(128 * half, 128 * half + 128)
            pairs[half, at] = both[:, lanes]
            pairs[2 + half, at] = k_both[:, lanes]

    each(1, 25, 2, fold)
    half = selector(256, 128, lambda r, c: r // 2 == c)
    for part, scale in ((0, 0.5), (1, 0.125)):
        both = jnp.concatenate([fold_rows(pairs, 2 * part, 192), fold_rows(pairs, 2 * part + 1, 192)], axis=1)
        c_out[part] = (pick(both, half) * scale).reshape(12, 16, 128)


def down1(first, own, second, ext, u, g, cx, cy, cz, dg, inv, c_out, k, d, w, pairs):
    at = lax.axis_index("gx")
    count = lax.axis_size("gx")
    lay_out(g, k, first, own, second, at // 2 % 2 == 0)

    @pl.when(at < 2)
    def _():
        for part, to in ((0, g), (1, k)):
            to[7:9] = ext[part, 0:2]

    @pl.when(at >= count - 2)
    def _():
        for part, to in ((0, g), (1, k)):
            to[17:19] = ext[part, 2:4]

    level = Level((u, g, cx, cy, cz, dg, inv, d, w), 6, False, True)
    level.from_zero(k, 1, 25, 3)

    def fold(planes):
        r = [r for _, r in level.remain(u, planes)]
        for i in range(0, len(planes), 2):
            at = rows_at((planes[i] - 3) // 2, 16)
            pairs[0, at] = (r[i] + r[i + 1])[8:24] * 0.5
            pairs[1, at] = (k[planes[i]] + k[planes[i + 1]])[8:24] * 0.125

    each(3, 23, 4, fold)
    half = selector(256, 128, lambda r, c: r // 2 == c)
    both = jnp.concatenate([fold_rows(pairs, 0, 80), fold_rows(pairs, 1, 80)], axis=1)
    c_out[...] = pick(both, half).reshape(10, 8, 128)


def down2(low, own, high, u, g, cx, cy, cz, dg, inv, c_out, k, d, w, pairs):
    at = lax.axis_index("gx")
    count = lax.axis_size("gx")
    parts = own.shape[0]
    rows = 8 * parts
    lane = lax.broadcasted_iota(jnp.int32, (rows, 128), 1)

    def plane(ref, p):
        return jnp.concatenate([ref[j, p] for j in range(parts)], axis=0)

    for i in range(22):
        if i < 6:
            v = plane(low, i)
        elif i == 6:
            v = jnp.where(at < 3, plane(own, 0), plane(low, 6))
        elif i < 15:
            v = plane(own, i - 6)
        elif i == 15:
            v = jnp.where(at >= count - 3, plane(own, 9), plane(high, 0))
        else:
            v = plane(high, i - 15)
        g[i + 1] = jnp.where(lane < 64, v, 0.0)
        k[i + 1] = jnp.where(lane < 64, pltpu.roll(v, 64, 1), 0.0)
    level = Level((u, g, cx, cy, cz, dg, inv, d, w), 4, True, False)
    level.from_zero(k, 1, 23, 3)

    def fold(planes):
        (_, r), (_, r_up) = level.remain(u, planes)
        k_both = (k[planes[0]] + k[planes[1]]) * 0.125
        both = jnp.where(lane < 64, (r + r_up) * 0.5, pltpu.roll(k_both, 64, 1))
        pairs[0, rows_at((planes[0] - 1) // 2, rows)] = both

    each(1, 23, 2, fold)
    half = selector(128, 128, lambda r, c: r // 2 == c)
    n = 11 * rows // 2
    both = pick(fold_rows(pairs, 0, n), half).reshape(11, rows // 2, 128)
    c_out[...] = both[:, :rows // 4] + pltpu.roll(both[:, rows // 4:], 64, 2)


def upward(first, own, second, *refs):
    at = lax.axis_index("gx")
    count = lax.axis_size("gx")
    gy = lax.axis_index("gy")
    s2, s1, s0 = refs[0:7], refs[7:14], refs[14:21]
    out, res = refs[21:23]
    s3, k3 = refs[23:32], refs[32]
    (start2, d2, w2), (start1, d1, w1), (start0, d0, w0) = refs[33:36], refs[36:39], refs[39:42]
    wide2, wide1, wide0, tall = refs[42:46]
    u3, g3 = s3[0:2]
    rows3 = 2 * own.shape[1]
    rows2 = 2 * rows3
    lane = lax.broadcasted_iota(jnp.int32, (rows3, 128), 1)
    even = at // 6 % 2 == 0
    for i in range(21):
        if i < 7:
            v = jnp.where(even, second[i], first[i])
            if i >= 5:
                v = jnp.where(at < 6, own[i - 5], v)
        elif i < 14:
            v = own[i - 5]
        else:
            v = jnp.where(even, first[i - 12], second[i - 12])
            if i < 16:
                v = jnp.where(at >= count - 6, own[i - 5], v)
        v = jnp.concatenate([v, pltpu.roll(v, 64, 1)], axis=0)
        g3[i + 1] = jnp.where(lane < 32, v, 0.0)
        k3[i + 1] = jnp.where(lane < 32, pltpu.roll(v, 96, 1), 0.0)
    level = Level(s3, 7, True, False)
    level.from_zero(k3, 1, 22, 6)
    spread = selector(128, 128, lambda r, c: c // 2 == r)

    fixed = []
    for p, (v, r) in zip(range(8, 15), level.remain(u3, list(range(8, 15)))):
        den = jnp.sum(level.dg[p], axis=0, keepdims=True)
        fix = jnp.sum(r, axis=0, keepdims=True) / jnp.where(den > 0.0, den, 1.0)
        fixed.append(v + jnp.where(k3[p] > 0.0, fix, 0.0))
    spread_rows(wide2, 0, pick(jnp.concatenate(fixed, axis=0), spread))
    level = Level((*s2, d2, w2), 4, True, False)
    for p in range(14):
        at = p // 2 * rows2
        start2[p] = level.u[p + 5] + wide2[0, at:at + rows2, :]
    u = level.from_start(start2, 0, 14, 3, 5)

    edge = jnp.zeros((8, 8, 128), F32)
    tall[:, 0:8, :] = edge
    tall[:, 8 + rows2:, :] = edge
    tall[:, 8:8 + rows2, :] = u[3:11]
    near = tall[:, pl.ds(pl.multiple_of(gy * 8, 8), 24), :][:, 4:20]
    spread_rows(wide1, 0, pick(near.reshape(128, 128), spread))
    level = Level((*s1, d1, w1), 4, False, True)
    for p in range(14):
        at = (p + 1) // 2 * 32
        start1[p] = level.u[p + 6] + wide1[0, at:at + 32, :]
    u = level.from_start(start1, 0, 14, 3, 6)

    wide = pick(u[3:11, 4:28, :].reshape(192, 128), selector(128, 256, lambda r, c: c // 2 == r))
    spread_rows(wide0, 0, wide[:, :128])
    spread_rows(wide0, 1, wide[:, 128:])
    level = Level((*s0, d0, w0), 4, False, True)

    def onto(i, carry):
        at = rows_at(i, 48)
        wide = jnp.concatenate([wide0[0, at], wide0[1, at]], axis=1)
        start0[2 * i] = level.u[2 * i + 5] + wide
        start0[2 * i + 1] = level.u[2 * i + 6] + wide
        return carry

    lax.fori_loop(0, 8, onto, 0)
    u = level.from_start(start0, 0, 16, 3, 5)

    def finish(planes):
        for p, (v, r) in zip(planes, level.remain(u, planes, 5)):
            out[p - 4] = v[8:40, :]
            res[p - 4] = r[8:40, :]

    each(4, 12, 2, finish)


def call(body, outs, scratch, name, limit):
    return pl.pallas_call(
        body,
        out_shape=[jax.ShapeDtypeStruct(shape, F32) for shape in outs],
        scratch_shapes=[pltpu.VMEM(shape, F32) for shape in scratch],
        compiler_params=pltpu.CompilerParams(vmem_limit_bytes=limit * 1024 * 1024),
        name=name,
    )


def swap(block, axis, step):
    count = lax.axis_size(axis)
    came = {}
    for side in (1, 0):
        pairs = [(t, t + step) for t in range(count - step) if t // step % 2 == side]
        came[side] = lax.ppermute(block, axis, pairs + [(b, a) for a, b in pairs])
    return came[0], came[1]


def shift(block, axis, step):
    count = lax.axis_size(axis)
    return lax.ppermute(block, axis, [(t, t + step) for t in range(count) if 0 <= t + step < count])


def shards(source, conduct):
    ny = lax.axis_size("gy")

    both = jnp.stack([source, conduct])
    both = jnp.concatenate([shift(both[:, :, 24:], "gy", 1), both, shift(both[:, :, :8], "gy", -1)], axis=2)
    first, second = swap(both, "gx", 1)
    plane = (26, 48, 256)
    *s0, c1 = call(
        down0, [plane] * 7 + [(2, 12, 16, 128)], [plane] * 3 + [(4, 384, 128)], "down0", 24,
    )(first, both, second)

    c1 = jnp.concatenate([shift(c1[:, :, 8:], "gy", 1), c1, shift(c1[:, :, :8], "gy", -1)], axis=2)
    window = c1[:, 2:10]
    ext = jnp.concatenate([c1[:, 0:2], c1[:, 10:12]], axis=1)
    first, second = swap(window, "gx", 2)
    plane = (26, 32, 128)
    *s1, c2 = call(
        down1, [plane] * 7 + [(10, 8, 128)], [plane] * 3 + [(2, 160, 128)], "down1", 12,
    )(first, window, second, ext)

    c2 = lax.all_to_all(jnp.broadcast_to(c2[None], (ny, 10, 8, 128)), "gy", 0, 0)
    rows = 8 * ny
    plane = (24, rows, 128)
    *s2, c3 = call(
        down2, [plane] * 7 + [(11, rows // 4, 128)], [plane] * 3 + [(1, 11 * rows, 128)], "down2", 20,
    )(shift(c2[:, 0:7], "gx", 3), c2, shift(c2[:, 3:10], "gx", -3))

    first, second = swap(c3[1:10], "gx", 6)
    out, res = call(
        upward, [(8, 32, 256)] * 2,
        [(23, rows // 2, 128)] * 10 + [(14, rows, 128)] * 3 + [(14, 32, 128)] * 3 + [(16, 48, 256)] * 3
        + [(1, 7 * rows, 128), (1, 256, 128), (2, 384, 128), (8, 16 + rows, 128)],
        "upward", 32,
    )(first, c3, second, *s2, *s1, *s0)
    return out, res


def solution(mesh):
    spec = P("gx", "gy", None)
    return jax.shard_map(shards, mesh=mesh, in_specs=(spec, spec), out_specs=(spec, spec), check_vma=False)
```

```python
import functools

import jax
import jax.numpy as jnp
from jax import lax
from jax.experimental import pallas as pl
from jax.experimental.pallas import tpu as pltpu
from jax.sharding import PartitionSpec as P

CENTER = 1.15
SPREAD = 0.85
RATIO = CENTER / SPREAD
F32 = jnp.float32
BF16 = jnp.bfloat16


def cheb_weights(degree):
    old = 1.0 / RATIO
    weights = []
    for _ in range(degree - 1):
        new = 1.0 / (2.0 * RATIO - old)
        weights.append((new * old, 2.0 * new / SPREAD))
        old = new
    return weights


def selector(rows, cols, test):
    r = lax.broadcasted_iota(jnp.int32, (rows, cols), 0)
    c = lax.broadcasted_iota(jnp.int32, (rows, cols), 1)
    return jnp.where(test(r, c), 1.0, 0.0).astype(BF16)


def pick(a, chosen):
    high = a.astype(BF16)
    rest = a - high.astype(F32)
    mid = rest.astype(BF16)
    low = (rest - mid.astype(F32)).astype(BF16)
    parts = [jnp.dot(part, chosen, preferred_element_type=F32) for part in (high, mid, low)]
    return parts[0] + (parts[1] + parts[2])


def each(lo, hi, block, body):
    whole = (hi - lo) // block

    def step(i, carry):
        p = lo + i * block
        body([p + b for b in range(block)])
        return carry

    if whole == 1:
        step(0, 0)
    else:
        lax.fori_loop(0, whole, step, 0)
    rest = list(range(lo + whole * block, hi))
    if rest:
        body(rest)


def next_row(v):
    return jnp.concatenate([v[1:], pltpu.roll(v[:1], 7, 1)], axis=0)


def last_row(v):
    return jnp.concatenate([pltpu.roll(v[-1:], 1, 1), v[:-1]], axis=0)


def rows_in(ref, *at, first=0, count=None):
    tall = (count or ref.shape[-2]) // 8
    tiles = [ref[(*at, pl.ds(first + t, 8, stride=tall), slice(None))] for t in range(tall)]
    return jnp.concatenate([tile[None] for tile in tiles], axis=0)


def rows_out(ref, *at, value, first=0):
    for t in range(value.shape[0]):
        ref[(*at, pl.ds(first + t, 8, stride=value.shape[0]), slice(None))] = value[t]


def fold_rows(v):
    v = v.reshape(v.shape[0] // 2, 2, *v.shape[1:])
    return v[:, 0] + v[:, 1]


def repeat_rows(v):
    return jnp.concatenate([v[t // 2][None] for t in range(2 * v.shape[0])], axis=0)


class Level:
    def __init__(self, refs, block, full_y, full_z):
        self.u, self.g, self.cx, self.cy, self.cz, self.dg, self.inv, self.d, self.w = refs
        self.block, self.full_y, self.full_z = block, full_y, full_z
        self.shape = self.d.shape[1:]
        self.lanes = self.shape[2]

    def from_zero(self, k_ref, lo, hi, degree):
        tall, _, lanes = self.shape
        zeros = jnp.zeros(self.shape, F32)
        for ref in (self.u, self.w, k_ref):
            ref[lo - 1] = zeros
            ref[hi] = zeros
        row = tall * lax.broadcasted_iota(jnp.int32, self.shape, 1) + lax.broadcasted_iota(jnp.int32, self.shape, 0)
        lane = lax.broadcasted_iota(jnp.int32, self.shape, 2)
        chain = [self.u, self.w] if degree % 2 else [self.w, self.u]
        targets = (self.cx, self.cy, self.cz, self.dg, self.inv, self.g, chain[0])

        def first(planes):
            k = [k_ref[p] for p in [planes[0] - 1] + planes + [planes[-1] + 1]]
            keep = []
            for at, p in enumerate(planes):
                back, own, up = k[at:at + 3]
                ky = next_row(own)
                kyb = last_row(own)
                kz = pltpu.roll(own, lanes - 1, 2)
                kzb = pltpu.roll(own, 1, 2)
                cy = 0.5 * (own + ky)
                cz = 0.5 * (own + kz)
                if self.full_y:
                    cy = jnp.where(row == 8 * tall - 1, 0.0, cy)
                    ky = jnp.where(row == 8 * tall - 1, 0.0, ky)
                    kyb = jnp.where(row == 0, 0.0, kyb)
                if self.full_z:
                    cz = jnp.where(lane == lanes - 1, 0.0, cz)
                    kz = jnp.where(lane == lanes - 1, 0.0, kz)
                    kzb = jnp.where(lane == 0, 0.0, kzb)
                dg = 3.0 * own + 0.5 * ((back + up) + (ky + kyb) + (kz + kzb))
                inside = own > 0.0
                inv = jnp.where(inside, 1.0 / jnp.where(inside, dg, 1.0), 0.0)
                g = self.g[p] * inv
                keep.append((0.5 * (own + up), cy, cz, dg, inv, g, g * (1.0 / CENTER)))
            for p, values in zip(planes, keep):
                for ref, value in zip(targets, values):
                    ref[p] = value

        self.cx[lo - 1] = 0.5 * k_ref[lo]
        each(lo, hi, self.block, first)
        for at, (a, b) in enumerate(cheb_weights(degree)):
            old, new = chain
            self.sweep(old, new, lo, hi, a, b, old if at == 0 else self.d, at < degree - 2)
            chain = [new, old]

    def from_start(self, start, lo, hi, degree, shift):
        chain = [start, self.w]
        for at, (a, b) in enumerate([(0.0, 1.0 / CENTER)] + cheb_weights(degree)):
            lo, hi = lo + 1, hi - 1
            old, new = chain
            self.sweep(old, new, lo, hi, a, b, self.d if at else None, at < degree - 1, shift)
            chain = [new, old]
        return chain[0]

    def sweep(self, old, new, lo, hi, a, b, before, keep, shift=0):
        def body(planes):
            values = []
            for p, (v, z) in zip(planes, self.scaled(old, planes, shift)):
                step = b * z
                if before is not None:
                    step = step + a * before[p]
                values.append((step, v + step))
            for p, (step, value) in zip(planes, values):
                if keep:
                    self.d[p] = step
                new[p] = value

        each(lo, hi, self.block, body)

    def scaled(self, u_ref, planes, shift=0):
        u = [u_ref[p] for p in [planes[0] - 1] + planes + [planes[-1] + 1]]
        cx = [self.cx[p + shift] for p in [planes[0] - 1] + planes]
        results = []
        for at, p in enumerate(planes):
            q = p + shift
            back, v, up = u[at:at + 3]
            cy = self.cy[q]
            cz = self.cz[q]
            s = cx[at + 1] * up + cx[at] * back
            s = s + (cy * next_row(v) + last_row(cy * v))
            s = s + (cz * pltpu.roll(v, self.lanes - 1, 2) + pltpu.roll(cz * v, 1, 2))
            results.append((v, (self.g[q] + s * self.inv[q]) - v))
        return results

    def remain(self, u_ref, planes, shift=0):
        return [(v, z * self.dg[p + shift]) for p, (v, z) in zip(planes, self.scaled(u_ref, planes, shift))]


def lay_out(g, k, first, own, second, even):
    half = own.shape[0] // 2

    def put(i, carry, start, ref):
        for part, to in ((0, g), (half, k)):
            value = [rows_in(ref, part + h, i) for h in range(half)]
            to[start + i] = jnp.concatenate(value, axis=2)
        return carry

    def planes(start, ref):
        lax.fori_loop(0, 8, functools.partial(put, start=start, ref=ref), 0)

    planes(9, own)

    @pl.when(even)
    def _():
        planes(1, second)
        planes(17, first)

    @pl.when(jnp.logical_not(even))
    def _():
        planes(1, first)
        planes(17, second)


def down0(first, own, second, u, g, cx, cy, cz, dg, inv, c_out, k, d, w, pairs):
    lay_out(g, k, first, own, second, lax.axis_index("gx") % 2 == 0)
    level = Level((u, g, cx, cy, cz, dg, inv, d, w), 4, False, True)
    level.from_zero(k, 1, 25, 3)

    def fold(planes):
        r = [r for _, r in level.remain(u, planes)]
        for i in range(0, len(planes), 2):
            both = fold_rows(r[i] + r[i + 1])
            k_both = fold_rows(k[planes[i]] + k[planes[i + 1]])
            at = (planes[i] - 1) // 2
            for half in range(2):
                lanes = slice(128 * half, 128 * half + 128)
                rows_out(pairs, half, at, value=both[:, :, lanes])
                rows_out(pairs, 2 + half, at, value=k_both[:, :, lanes])

    each(1, 25, 4, fold)
    half = selector(256, 128, lambda r, c: r // 2 == c)
    for part, scale in ((0, 0.5), (1, 0.125)):
        both = [pairs[2 * part + h][:, 4:20].reshape(192, 128) for h in range(2)]
        c_out[part] = (pick(jnp.concatenate(both, axis=1), half) * scale).reshape(12, 16, 128)


def down1(first, own, second, ext, u, g, cx, cy, cz, dg, inv, c_out, k, d, w, pairs):
    at = lax.axis_index("gx")
    count = lax.axis_size("gx")
    lay_out(g, k, first, own, second, at // 2 % 2 == 0)

    @pl.when(at < 2)
    def _():
        for part, to in ((0, g), (1, k)):
            for i in range(2):
                to[7 + i] = rows_in(ext, part, i)

    @pl.when(at >= count - 2)
    def _():
        for part, to in ((0, g), (1, k)):
            for i in range(2):
                to[17 + i] = rows_in(ext, part, 2 + i)

    level = Level((u, g, cx, cy, cz, dg, inv, d, w), 6, False, True)
    level.from_zero(k, 1, 25, 3)

    def fold(planes):
        r = [r for _, r in level.remain(u, planes)]
        for i in range(0, len(planes), 2):
            at = (planes[i] - 3) // 2
            rows_out(pairs, 0, at, value=fold_rows(r[i] + r[i + 1]) * 0.5)
            rows_out(pairs, 1, at, value=fold_rows(k[planes[i]] + k[planes[i + 1]]) * 0.125)

    each(3, 23, 4, fold)
    half = selector(256, 128, lambda r, c: r // 2 == c)
    both = [pairs[part][:, 4:12].reshape(80, 128) for part in range(2)]
    c_out[...] = pick(jnp.concatenate(both, axis=1), half).reshape(10, 8, 128)


def down2(low, own, high, u, g, cx, cy, cz, dg, inv, c_out, k, d, w, pairs, flat):
    at = lax.axis_index("gx")
    count = lax.axis_size("gx")
    parts = own.shape[0]
    lane = lax.broadcasted_iota(jnp.int32, u.shape[1:], 2)

    for i in range(22):
        for j in range(parts):
            if i < 6:
                v = low[j, i]
            elif i == 6:
                v = jnp.where(at < 3, own[j, 0], low[j, 6])
            elif i < 15:
                v = own[j, i - 6]
            elif i == 15:
                v = jnp.where(at >= count - 3, own[j, 9], high[j, 0])
            else:
                v = high[j, i - 15]
            flat[i, 8 * j:8 * j + 8] = v

    def lay(planes):
        values = [rows_in(flat, p - 1) for p in planes]
        for p, v in zip(planes, values):
            g[p] = jnp.where(lane < 64, v, 0.0)
            k[p] = jnp.where(lane < 64, pltpu.roll(v, 64, 2), 0.0)

    each(1, 23, 2, lay)
    level = Level((u, g, cx, cy, cz, dg, inv, d, w), 4, True, False)
    level.from_zero(k, 1, 23, 3)
    short = lax.broadcasted_iota(jnp.int32, (parts // 2, 8, 128), 2)

    def fold(planes):
        r = [r for _, r in level.remain(u, planes)]
        for i in range(0, len(planes), 2):
            k_both = fold_rows(k[planes[i]] + k[planes[i + 1]]) * 0.125
            both = fold_rows(r[i] + r[i + 1]) * 0.5
            rows_out(pairs, (planes[i] - 1) // 2, value=jnp.where(short < 64, both, pltpu.roll(k_both, 64, 2)))

    each(1, 23, 2, fold)
    half = selector(128, 128, lambda r, c: r // 2 == c)
    rows = 4 * parts
    both = pick(pairs[...].reshape(11 * rows, 128), half).reshape(11, rows, 128)
    c_out[...] = both[:, :rows // 2] + pltpu.roll(both[:, rows // 2:], 64, 2)


def upward(first, own, second, *refs):
    at = lax.axis_index("gx")
    count = lax.axis_size("gx")
    gy = lax.axis_index("gy")
    s2, s1, s0 = refs[0:7], refs[7:14], refs[14:21]
    out, res = refs[21:23]
    s3, k3 = refs[23:32], refs[32]
    (start2, d2, w2), (start1, d1, w1), (start0, d0, w0) = refs[33:36], refs[36:39], refs[39:42]
    flat3, tall, near, flat1, flat0 = refs[42:47]
    u3, g3 = s3[0:2]
    rows3 = 2 * own.shape[1]
    lane = lax.broadcasted_iota(jnp.int32, u3.shape[1:], 2)
    even = at // 6 % 2 == 0
    for i in range(21):
        if i < 7:
            v = jnp.where(even, second[i], first[i])
            if i >= 5:
                v = jnp.where(at < 6, own[i - 5], v)
        elif i < 14:
            v = own[i - 5]
        else:
            v = jnp.where(even, first[i - 12], second[i - 12])
            if i < 16:
                v = jnp.where(at >= count - 6, own[i - 5], v)
        flat3[i] = jnp.concatenate([v, pltpu.roll(v, 64, 1)], axis=0)

    def lay(planes):
        values = [rows_in(flat3, p - 1) for p in planes]
        for p, v in zip(planes, values):
            g3[p] = jnp.where(lane < 32, v, 0.0)
            k3[p] = jnp.where(lane < 32, pltpu.roll(v, 96, 2), 0.0)

    each(1, 22, 3, lay)
    level = Level(s3, 7, True, False)
    level.from_zero(k3, 1, 22, 6)
    spread = selector(128, 128, lambda r, c: c // 2 == r)

    fixed = []
    for p, (v, r) in zip(range(8, 15), level.remain(u3, list(range(8, 15)))):
        den = jnp.sum(level.dg[p], axis=(0, 1), keepdims=True)
        fix = jnp.sum(r, axis=(0, 1), keepdims=True) / jnp.where(den > 0.0, den, 1.0)
        fixed.append(v + jnp.where(k3[p] > 0.0, fix, 0.0))
    wide = pick(jnp.concatenate(fixed, axis=0).reshape(7 * rows3, 128), spread)
    wide = wide.reshape(7, rows3 // 8, 8, 128)
    level = Level((*s2, d2, w2), 4, True, False)
    for i in range(7):
        both = repeat_rows(wide[i])
        start2[2 * i] = level.u[2 * i + 5] + both
        start2[2 * i + 1] = level.u[2 * i + 6] + both
    u = level.from_start(start2, 0, 14, 3, 5)

    edge = jnp.zeros((8, 8, 128), F32)
    tall[:, 0:8, :] = edge
    tall[:, 8 + 2 * rows3:, :] = edge
    for i in range(8):
        rows_out(tall, i, value=u[i + 3], first=8)
    near[...] = tall[:, pl.ds(pl.multiple_of(gy * 8, 8), 24), :]
    wide = jnp.concatenate([rows_in(near, i, first=4, count=16) for i in range(8)], axis=0)
    wide = pick(wide.reshape(128, 128), spread).reshape(8, 2, 8, 128)
    level = Level((*s1, d1, w1), 4, False, True)
    for p in range(14):
        start1[p] = level.u[p + 6] + repeat_rows(wide[(p + 1) // 2])
    u = level.from_start(start1, 0, 14, 3, 6)

    for i in range(8):
        rows_out(flat1, i, value=u[i + 3])
    wide = jnp.concatenate([rows_in(flat1, i, first=4, count=24) for i in range(8)], axis=0)
    wide = pick(wide.reshape(192, 128), selector(128, 256, lambda r, c: c // 2 == r)).reshape(8, 3, 8, 256)
    level = Level((*s0, d0, w0), 4, False, True)
    for i in range(8):
        both = repeat_rows(wide[i])
        start0[2 * i] = level.u[2 * i + 5] + both
        start0[2 * i + 1] = level.u[2 * i + 6] + both
    u = level.from_start(start0, 0, 16, 3, 5)

    def finish(planes):
        for i, (p, values) in enumerate(zip(planes, level.remain(u, planes, 5))):
            for which, to in ((0, out), (1, res)):
                for half in range(2):
                    lanes = slice(128 * half, 128 * half + 128)
                    rows_out(flat0, which, half, i, value=values[which][:, :, lanes])
                    to[p - 4, :, lanes] = flat0[which, half, i, 8:40]

    each(4, 12, 4, finish)


def call(body, outs, scratch, name, limit):
    return pl.pallas_call(
        body,
        out_shape=[jax.ShapeDtypeStruct(shape, F32) for shape in outs],
        scratch_shapes=[pltpu.VMEM(shape, F32) for shape in scratch],
        compiler_params=pltpu.CompilerParams(vmem_limit_bytes=limit * 1024 * 1024),
        name=name,
    )


def swap(block, axis, step):
    count = lax.axis_size(axis)
    came = {}
    for side in (1, 0):
        pairs = [(t, t + step) for t in range(count - step) if t // step % 2 == side]
        came[side] = lax.ppermute(block, axis, pairs + [(b, a) for a, b in pairs])
    return came[0], came[1]


def shift(block, axis, step):
    count = lax.axis_size(axis)
    return lax.ppermute(block, axis, [(t, t + step) for t in range(count) if 0 <= t + step < count])


def shards(source, conduct):
    ny = lax.axis_size("gy")

    both = jnp.stack([array[:, :, lanes] for array in (source, conduct) for lanes in (slice(0, 128), slice(128, 256))])
    both = jnp.concatenate([shift(both[:, :, 24:], "gy", 1), both, shift(both[:, :, :8], "gy", -1)], axis=2)
    first, second = swap(both, "gx", 1)
    plane = (26, 6, 8, 256)
    *s0, c1 = call(
        down0, [plane] * 7 + [(2, 12, 16, 128)], [plane] * 3 + [(4, 12, 24, 128)], "down0", 24,
    )(first, both, second)

    c1 = jnp.concatenate([shift(c1[:, :, 8:], "gy", 1), c1, shift(c1[:, :, :8], "gy", -1)], axis=2)
    window = c1[:, 2:10]
    ext = jnp.concatenate([c1[:, 0:2], c1[:, 10:12]], axis=1)
    first, second = swap(window, "gx", 2)
    plane = (26, 4, 8, 128)
    *s1, c2 = call(
        down1, [plane] * 7 + [(10, 8, 128)], [plane] * 3 + [(2, 10, 16, 128)], "down1", 12,
    )(first, window, second, ext)

    c2 = lax.all_to_all(jnp.broadcast_to(c2[None], (ny, 10, 8, 128)), "gy", 0, 0)
    rows = 8 * ny
    plane = (24, ny, 8, 128)
    *s2, c3 = call(
        down2, [plane] * 7 + [(11, rows // 4, 128)], [plane] * 3 + [(11, rows // 2, 128), (22, rows, 128)], "down2", 20,
    )(shift(c2[:, 0:7], "gx", 3), c2, shift(c2[:, 3:10], "gx", -3))

    first, second = swap(c3[1:10], "gx", 6)
    out, res = call(
        upward, [(8, 32, 256)] * 2,
        [(23, ny // 2, 8, 128)] * 10 + [(14, ny, 8, 128)] * 3 + [(14, 4, 8, 128)] * 3 + [(16, 6, 8, 256)] * 3
        + [(21, rows // 2, 128), (8, 16 + rows, 128), (8, 24, 128), (8, 32, 128), (2, 2, 4, 48, 128)],
        "upward", 32,
    )(first, c3, second, *s2, *s1, *s0)
    return out, res


def solution(mesh):
    spec = P("gx", "gy", None)
    return jax.shard_map(shards, mesh=mesh, in_specs=(spec, spec), out_specs=(spec, spec), check_vma=False)
```

```python
import functools

import jax
import jax.numpy as jnp
from jax import lax
from jax.experimental import pallas as pl
from jax.experimental.pallas import tpu as pltpu
from jax.sharding import PartitionSpec as P

CENTER = 1.15
SPREAD = 0.85
RATIO = CENTER / SPREAD
F32 = jnp.float32
BF16 = jnp.bfloat16


def cheb_weights(degree):
    old = 1.0 / RATIO
    weights = []
    for _ in range(degree - 1):
        new = 1.0 / (2.0 * RATIO - old)
        weights.append((new * old, 2.0 * new / SPREAD))
        old = new
    return weights


def selector(rows, cols, test):
    r = lax.broadcasted_iota(jnp.int32, (rows, cols), 0)
    c = lax.broadcasted_iota(jnp.int32, (rows, cols), 1)
    return jnp.where(test(r, c), 1.0, 0.0).astype(BF16)


def pick(a, chosen):
    high = a.astype(BF16)
    rest = a - high.astype(F32)
    mid = rest.astype(BF16)
    low = (rest - mid.astype(F32)).astype(BF16)
    parts = [jnp.dot(part, chosen, preferred_element_type=F32) for part in (high, mid, low)]
    return parts[0] + (parts[1] + parts[2])


def each(lo, hi, block, body):
    whole = (hi - lo) // block

    def step(i, carry):
        p = lo + i * block
        body([p + b for b in range(block)])
        return carry

    if whole == 1:
        step(0, 0)
    else:
        lax.fori_loop(0, whole, step, 0)
    rest = list(range(lo + whole * block, hi))
    if rest:
        body(rest)


def next_row(v):
    if v.ndim == 2:
        return pltpu.roll(v, v.shape[0] - 1, 0)
    return jnp.concatenate([v[1:], pltpu.roll(v[:1], 7, 1)], axis=0)


def last_row(v):
    if v.ndim == 2:
        return pltpu.roll(v, 1, 0)
    return jnp.concatenate([pltpu.roll(v[-1:], 1, 1), v[:-1]], axis=0)


def next_lane(v):
    return pltpu.roll(v, v.shape[-1] - 1, v.ndim - 1)


def last_lane(v):
    return pltpu.roll(v, 1, v.ndim - 1)


def rows_in(ref, *at, first=0, count=None):
    tall = (count or ref.shape[-2]) // 8
    tiles = [ref[(*at, pl.ds(first + t, 8, stride=tall), slice(None))] for t in range(tall)]
    return jnp.concatenate([tile[None] for tile in tiles], axis=0)


def rows_out(ref, *at, value):
    for t in range(value.shape[0]):
        ref[(*at, pl.ds(t, 8, stride=value.shape[0]), slice(None))] = value[t]


def fold_tiles(v):
    v = v.reshape(v.shape[0] // 2, 2, *v.shape[1:])
    return v[:, 0] + v[:, 1]


class Level:
    def __init__(self, refs, block, full_y, full_z):
        self.u, self.g, self.cx, self.cy, self.cz, self.dg, self.inv, self.w = refs
        self.block, self.full_y, self.full_z = block, full_y, full_z
        self.shape = self.w.shape[1:]

    def from_zero(self, k_ref, lo, hi, degree, trim):
        lanes = self.shape[-1]
        zeros = jnp.zeros(self.shape, F32)
        for ref in (self.u, self.w, k_ref):
            ref[lo - 1] = zeros
            ref[hi] = zeros
        if self.full_y:
            row = lax.broadcasted_iota(jnp.int32, self.shape, 0)
        lane = lax.broadcasted_iota(jnp.int32, self.shape, len(self.shape) - 1)
        chain = [self.u, self.w] if degree % 2 else [self.w, self.u]
        targets = (self.cx, self.cy, self.cz, self.dg, self.inv, self.g, chain[0])

        def faces(planes):
            k = [k_ref[p] for p in [planes[0] - 1] + planes + [planes[-1] + 1]]
            keep = []
            for at, p in enumerate(planes):
                back, own, up = k[at:at + 3]
                ky, kyb, kz, kzb = next_row(own), last_row(own), next_lane(own), last_lane(own)
                cy = 0.5 * (own + ky)
                cz = 0.5 * (own + kz)
                if self.full_y:
                    cy = jnp.where(row == self.shape[0] - 1, 0.0, cy)
                    ky = jnp.where(row == self.shape[0] - 1, 0.0, ky)
                    kyb = jnp.where(row == 0, 0.0, kyb)
                if self.full_z:
                    cz = jnp.where(lane == lanes - 1, 0.0, cz)
                    kz = jnp.where(lane == lanes - 1, 0.0, kz)
                    kzb = jnp.where(lane == 0, 0.0, kzb)
                dg = 3.0 * own + 0.5 * ((back + up) + (ky + kyb) + (kz + kzb))
                inside = own > 0.0
                inv = jnp.where(inside, 1.0 / jnp.where(inside, dg, 1.0), 0.0)
                g = self.g[p] * inv
                keep.append((0.5 * (own + up), cy, cz, dg, inv, g, g * (1.0 / CENTER)))
            for p, values in zip(planes, keep):
                for ref, value in zip(targets, values):
                    ref[p] = value

        lo, hi = lo + trim, hi - trim
        self.cx[lo - 1] = 0.5 * (k_ref[lo - 1] + k_ref[lo])
        each(lo, hi, self.block, faces)
        for at, (a, b) in enumerate(cheb_weights(degree)):
            lo, hi = lo + trim, hi - trim
            self.sweep(*chain, lo, hi, a, b, at == 0)
            chain.reverse()

    def from_start(self, start, lo, hi, degree, shift):
        chain = [start, self.w]
        for a, b in [(0.0, 1.0 / CENTER)] + cheb_weights(degree):
            lo, hi = lo + 1, hi - 1
            self.sweep(*chain, lo, hi, a, b, a == 0.0, shift)
            chain.reverse()
        return chain[0]

    def sweep(self, old, new, lo, hi, a, b, first, shift=0):
        def body(planes):
            values = []
            for p, (v, z) in zip(planes, self.scaled(old, planes, shift)):
                value = (1.0 + a) * v + b * z if a else v + b * z
                values.append(value if first else value - a * new[p])
            for p, value in zip(planes, values):
                new[p] = value

        each(lo, hi, self.block, body)

    def scaled(self, u_ref, planes, shift=0):
        u = [u_ref[p] for p in [planes[0] - 1] + planes + [planes[-1] + 1]]
        cx = [self.cx[p + shift] for p in [planes[0] - 1] + planes]
        results = []
        for at, p in enumerate(planes):
            q = p + shift
            back, v, up = u[at:at + 3]
            cy = self.cy[q]
            cz = self.cz[q]
            s = cx[at + 1] * up + cx[at] * back
            s = s + (cy * next_row(v) + last_row(cy * v))
            s = s + (cz * next_lane(v) + last_lane(cz * v))
            results.append((v, (self.g[q] + s * self.inv[q]) - v))
        return results

    def remain(self, u_ref, planes, shift=0):
        return [(v, z * self.dg[p + shift]) for p, (v, z) in zip(planes, self.scaled(u_ref, planes, shift))]


def fold_rows(ref, at, count):
    return ref[at, pl.ds(0, count, stride=2), :] + ref[at, pl.ds(1, count, stride=2), :]


def spread_rows(ref, at, value):
    count = value.shape[0]
    ref[at, pl.ds(0, count, stride=2), :] = value
    ref[at, pl.ds(1, count, stride=2), :] = value


def rows_at(i, count):
    return pl.ds(pl.multiple_of(i * count, count), count)


def by_place(reach, run):
    at = lax.axis_index("gx")
    edge = (at < reach) | (at >= lax.axis_size("gx") - reach)
    pl.when(edge)(lambda: run(0))
    pl.when(jnp.logical_not(edge))(lambda: run(1))


def take_sides(even, first, second, put):
    @pl.when(even)
    def _():
        put(1, second)
        put(17, first)

    @pl.when(jnp.logical_not(even))
    def _():
        put(1, first)
        put(17, second)


def down0(first, own, second, u, g, cx, cy, cz, dg, inv, c_out, k, w, pairs):
    def put(start, ref):
        def plane(i, carry):
            for part, to in ((0, g), (2, k)):
                to[start + i] = jnp.concatenate([rows_in(ref, part + half, i) for half in range(2)], axis=2)
            return carry

        lax.fori_loop(0, 8, plane, 0)

    put(9, own)
    take_sides(lax.axis_index("gx") % 2 == 0, first, second, put)
    level = Level((u, g, cx, cy, cz, dg, inv, w), 4, False, True)

    def keep(at, first, both):
        for half in range(2):
            rows_out(pairs, first + half, at, value=both[:, :, 128 * half:128 * half + 128])

    def fold_k(planes):
        for p in planes[::2]:
            keep((p - 1) // 2, 2, fold_tiles(k[p] + k[p + 1]))

    def fold(planes):
        r = [r for _, r in level.remain(u, planes)]
        for i in range(0, len(planes), 2):
            keep((planes[i] - 1) // 2, 0, fold_tiles(r[i] + r[i + 1]))

    def run(trim):
        level.from_zero(k, 1, 25, 3, trim)
        if trim:
            pairs[0:2] = jnp.zeros((2, 12, 24, 128), F32)
        each(1 + 4 * trim, 25 - 4 * trim, 4, fold)

    by_place(2, run)
    each(1, 25, 4, fold_k)
    half = selector(256, 128, lambda r, c: r // 2 == c)
    for part, scale in ((0, 0.5), (1, 0.125)):
        both = [pairs[2 * part + h][:, 4:20].reshape(192, 128) for h in range(2)]
        c_out[part] = (pick(jnp.concatenate(both, axis=1), half) * scale).reshape(12, 16, 128)


def down1(first, own, second, ext, u, g, cx, cy, cz, dg, inv, c_out, k, w, pairs):
    at = lax.axis_index("gx")
    count = lax.axis_size("gx")

    def put(start, ref):
        for part, to in ((0, g), (1, k)):
            to[start:start + 8] = ref[part]

    put(9, own)
    take_sides(at // 2 % 2 == 0, first, second, put)

    @pl.when(at < 2)
    def _():
        for part, to in ((0, g), (1, k)):
            to[7:9] = ext[part, 0:2]

    @pl.when(at >= count - 2)
    def _():
        for part, to in ((0, g), (1, k)):
            to[17:19] = ext[part, 2:4]

    level = Level((u, g, cx, cy, cz, dg, inv, w), 6, False, True)

    def fold_k(planes):
        for p in planes[::2]:
            pairs[1, rows_at((p - 3) // 2, 16)] = (k[p] + k[p + 1])[8:24] * 0.125

    def fold(planes):
        r = [r for _, r in level.remain(u, planes)]
        for i in range(0, len(planes), 2):
            pairs[0, rows_at((planes[i] - 3) // 2, 16)] = (r[i] + r[i + 1])[8:24] * 0.5

    def run(trim):
        level.from_zero(k, 1, 25, 3, trim)
        if trim:
            pairs[0, 0:16] = jnp.zeros((16, 128), F32)
            pairs[0, 144:160] = jnp.zeros((16, 128), F32)
        each(3 + 2 * trim, 23 - 2 * trim, 4, fold)

    by_place(3, run)
    each(3, 23, 4, fold_k)
    half = selector(256, 128, lambda r, c: r // 2 == c)
    both = jnp.concatenate([fold_rows(pairs, 0, 80), fold_rows(pairs, 1, 80)], axis=1)
    c_out[...] = pick(both, half).reshape(10, 8, 128)


def down2(low, own, high, u, g, cx, cy, cz, dg, inv, c_out, k, w, pairs):
    at = lax.axis_index("gx")
    count = lax.axis_size("gx")
    parts = own.shape[0]
    rows = 8 * parts
    lane = lax.broadcasted_iota(jnp.int32, (rows, 128), 1)

    def plane(ref, p):
        return jnp.concatenate([ref[j, p] for j in range(parts)], axis=0)

    for i in range(22):
        if i < 6:
            v = plane(low, i)
        elif i == 6:
            v = jnp.where(at < 3, plane(own, 0), plane(low, 6))
        elif i < 15:
            v = plane(own, i - 6)
        elif i == 15:
            v = jnp.where(at >= count - 3, plane(own, 9), plane(high, 0))
        else:
            v = plane(high, i - 15)
        g[i + 1] = jnp.where(lane < 64, v, 0.0)
        k[i + 1] = jnp.where(lane < 64, pltpu.roll(v, 64, 1), 0.0)
    level = Level((u, g, cx, cy, cz, dg, inv, w), 4, True, False)

    def keep(p, both, k_both):
        pairs[0, rows_at((p - 1) // 2, rows)] = jnp.where(lane < 64, both, pltpu.roll(k_both * 0.125, 64, 1))

    def fold_k(planes):
        for p in planes[::2]:
            keep(p, 0.0, k[p] + k[p + 1])

    def fold(planes):
        r = [r for _, r in level.remain(u, planes)]
        for i in range(0, len(planes), 2):
            keep(planes[i], (r[i] + r[i + 1]) * 0.5, k[planes[i]] + k[planes[i] + 1])

    def run(trim):
        level.from_zero(k, 1, 23, 3, trim)
        each(1 + 4 * trim, 23 - 4 * trim, 2, fold)
        if trim:
            each(1, 5, 4, fold_k)
            each(19, 23, 4, fold_k)

    by_place(6, run)
    half = selector(128, 128, lambda r, c: r // 2 == c)
    n = 11 * rows // 2
    both = pick(fold_rows(pairs, 0, n), half).reshape(11, rows // 2, 128)
    c_out[...] = both[:, :rows // 4] + pltpu.roll(both[:, rows // 4:], 64, 2)


def upward(first, own, second, *refs):
    at = lax.axis_index("gx")
    count = lax.axis_size("gx")
    gy = lax.axis_index("gy")
    s2, s1, s0 = refs[0:7], refs[7:14], refs[14:21]
    out, res = refs[21:23]
    s3, k3 = refs[23:31], refs[31]
    (start2, w2), (start1, w1), (start0, w0) = refs[32:34], refs[34:36], refs[36:38]
    wide2, wide1, flat0, tall = refs[38:42]
    u3, g3 = s3[0:2]
    rows3 = 2 * own.shape[1]
    rows2 = 2 * rows3
    lane = lax.broadcasted_iota(jnp.int32, (rows3, 128), 1)
    even = at // 6 % 2 == 0
    for i in range(21):
        if i < 7:
            v = jnp.where(even, second[i], first[i])
            if i >= 5:
                v = jnp.where(at < 6, own[i - 5], v)
        elif i < 14:
            v = own[i - 5]
        else:
            v = jnp.where(even, first[i - 12], second[i - 12])
            if i < 16:
                v = jnp.where(at >= count - 6, own[i - 5], v)
        v = jnp.concatenate([v, pltpu.roll(v, 64, 1)], axis=0)
        g3[i + 1] = jnp.where(lane < 32, v, 0.0)
        k3[i + 1] = jnp.where(lane < 32, pltpu.roll(v, 96, 1), 0.0)
    level = Level(s3, 7, True, False)
    level.from_zero(k3, 1, 22, 6, 1)
    spread = selector(128, 128, lambda r, c: c // 2 == r)

    fixed = []
    for p, (v, r) in zip(range(8, 15), level.remain(u3, list(range(8, 15)))):
        den = jnp.sum(level.dg[p], axis=0, keepdims=True)
        fix = jnp.sum(r, axis=0, keepdims=True) / jnp.where(den > 0.0, den, 1.0)
        fixed.append(v + jnp.where(k3[p] > 0.0, fix, 0.0))
    spread_rows(wide2, 0, pick(jnp.concatenate(fixed, axis=0), spread))
    level = Level((*s2, w2), 4, True, False)
    for p in range(14):
        at = p // 2 * rows2
        start2[p] = level.u[p + 5] + wide2[0, at:at + rows2, :]
    u = level.from_start(start2, 0, 14, 3, 5)

    edge = jnp.zeros((8, 8, 128), F32)
    tall[:, 0:8, :] = edge
    tall[:, 8 + rows2:, :] = edge
    tall[:, 8:8 + rows2, :] = u[3:11]
    near = tall[:, pl.ds(pl.multiple_of(gy * 8, 8), 24), :][:, 4:20]
    spread_rows(wide1, 0, pick(near.reshape(128, 128), spread))
    level = Level((*s1, w1), 4, False, True)
    for p in range(14):
        at = (p + 1) // 2 * 32
        start1[p] = level.u[p + 6] + wide1[0, at:at + 32, :]
    u = level.from_start(start1, 0, 14, 3, 6)

    wide = jnp.concatenate([rows_in(u, i + 3, first=4, count=24) for i in range(8)], axis=0)
    wide = pick(wide.reshape(192, 128), selector(128, 256, lambda r, c: c // 2 == r)).reshape(8, 3, 8, 256)
    level = Level((*s0, w0), 4, False, True)
    for i in range(8):
        both = jnp.concatenate([wide[i, t // 2][None] for t in range(6)], axis=0)
        start0[2 * i] = level.u[2 * i + 5] + both
        start0[2 * i + 1] = level.u[2 * i + 6] + both
    u = level.from_start(start0, 0, 16, 3, 5)

    def finish(planes):
        for i, (p, values) in enumerate(zip(planes, level.remain(u, planes, 5))):
            for which, to in ((0, out), (1, res)):
                for half in range(2):
                    lanes = slice(128 * half, 128 * half + 128)
                    rows_out(flat0, which, half, i, value=values[which][:, :, lanes])
                    to[p - 4, :, lanes] = flat0[which, half, i, 8:40]

    each(4, 12, 4, finish)


def call(body, outs, scratch, name, limit):
    return pl.pallas_call(
        body,
        out_shape=[jax.ShapeDtypeStruct(shape, F32) for shape in outs],
        scratch_shapes=[pltpu.VMEM(shape, F32) for shape in scratch],
        compiler_params=pltpu.CompilerParams(vmem_limit_bytes=limit * 1024 * 1024),
        name=name,
    )


def swap(block, axis, step):
    count = lax.axis_size(axis)
    came = {}
    for side in (1, 0):
        pairs = [(t, t + step) for t in range(count - step) if t // step % 2 == side]
        came[side] = lax.ppermute(block, axis, pairs + [(b, a) for a, b in pairs])
    return came[0], came[1]


def shift(block, axis, step):
    count = lax.axis_size(axis)
    return lax.ppermute(block, axis, [(t, t + step) for t in range(count) if 0 <= t + step < count])


def shards(source, conduct):
    ny = lax.axis_size("gy")

    both = jnp.stack([array[:, :, lanes] for array in (source, conduct) for lanes in (slice(0, 128), slice(128, 256))])
    both = jnp.concatenate([shift(both[:, :, 24:], "gy", 1), both, shift(both[:, :, :8], "gy", -1)], axis=2)
    first, second = swap(both, "gx", 1)
    plane = (26, 6, 8, 256)
    *s0, c1 = call(
        down0, [plane] * 7 + [(2, 12, 16, 128)], [plane] * 2 + [(4, 12, 24, 128)], "down0", 24,
    )(first, both, second)

    c1 = jnp.concatenate([shift(c1[:, :, 8:], "gy", 1), c1, shift(c1[:, :, :8], "gy", -1)], axis=2)
    window = c1[:, 2:10]
    ext = jnp.concatenate([c1[:, 0:2], c1[:, 10:12]], axis=1)
    first, second = swap(window, "gx", 2)
    plane = (26, 32, 128)
    *s1, c2 = call(
        down1, [plane] * 7 + [(10, 8, 128)], [plane] * 2 + [(2, 160, 128)], "down1", 12,
    )(first, window, second, ext)

    c2 = lax.all_to_all(jnp.broadcast_to(c2[None], (ny, 10, 8, 128)), "gy", 0, 0)
    rows = 8 * ny
    plane = (24, rows, 128)
    *s2, c3 = call(
        down2, [plane] * 7 + [(11, rows // 4, 128)], [plane] * 2 + [(1, 11 * rows, 128)], "down2", 20,
    )(shift(c2[:, 0:7], "gx", 3), c2, shift(c2[:, 3:10], "gx", -3))

    first, second = swap(c3[1:10], "gx", 6)
    out, res = call(
        upward, [(8, 32, 256)] * 2,
        [(23, rows // 2, 128)] * 9 + [(14, rows, 128)] * 2 + [(14, 32, 128)] * 2 + [(16, 6, 8, 256)] * 2
        + [(1, 7 * rows, 128), (1, 256, 128), (2, 2, 4, 48, 128), (8, 16 + rows, 128)],
        "upward", 32,
    )(first, c3, second, *s2, *s1, *s0)
    return out, res


def solution(mesh):
    spec = P("gx", "gy", None)
    return jax.shard_map(shards, mesh=mesh, in_specs=(spec, spec), out_specs=(spec, spec), check_vma=False)
```

```python
import functools

import jax
import jax.numpy as jnp
from jax import lax
from jax.experimental import pallas as pl
from jax.experimental.pallas import tpu as pltpu
from jax.sharding import PartitionSpec as P

CENTER = 1.15
SPREAD = 0.85
RATIO = CENTER / SPREAD
F32 = jnp.float32
BF16 = jnp.bfloat16


def cheb_weights(degree):
    old = 1.0 / RATIO
    weights = []
    for _ in range(degree - 1):
        new = 1.0 / (2.0 * RATIO - old)
        weights.append((new * old, 2.0 * new / SPREAD))
        old = new
    return weights


def selector(rows, cols, test):
    r = lax.broadcasted_iota(jnp.int32, (rows, cols), 0)
    c = lax.broadcasted_iota(jnp.int32, (rows, cols), 1)
    return jnp.where(test(r, c), 1.0, 0.0).astype(BF16)


def pick(a, chosen):
    high = a.astype(BF16)
    rest = a - high.astype(F32)
    mid = rest.astype(BF16)
    low = (rest - mid.astype(F32)).astype(BF16)
    parts = [jnp.dot(part, chosen, preferred_element_type=F32) for part in (high, mid, low)]
    return parts[0] + (parts[1] + parts[2])


def each(lo, hi, block, body):
    whole = (hi - lo) // block

    def step(i, carry):
        p = lo + i * block
        body([p + b for b in range(block)])
        return carry

    if whole == 1:
        step(0, 0)
    else:
        lax.fori_loop(0, whole, step, 0)
    rest = list(range(lo + whole * block, hi))
    if rest:
        body(rest)


def next_row(v):
    if v.ndim == 2:
        return pltpu.roll(v, v.shape[0] - 1, 0)
    return jnp.concatenate([v[1:], pltpu.roll(v[:1], 7, 1)], axis=0)


def last_row(v):
    if v.ndim == 2:
        return pltpu.roll(v, 1, 0)
    return jnp.concatenate([pltpu.roll(v[-1:], 1, 1), v[:-1]], axis=0)


def next_lane(v):
    return pltpu.roll(v, v.shape[-1] - 1, v.ndim - 1)


def last_lane(v):
    return pltpu.roll(v, 1, v.ndim - 1)


def rows_in(ref, *at, first=0, count=None):
    tall = (count or ref.shape[-2]) // 8
    tiles = [ref[(*at, pl.ds(first + t, 8, stride=tall), slice(None))] for t in range(tall)]
    return jnp.concatenate([tile[None] for tile in tiles], axis=0)


def rows_out(ref, *at, value):
    for t in range(value.shape[0]):
        ref[(*at, pl.ds(t, 8, stride=value.shape[0]), slice(None))] = value[t]


def fold_tiles(v):
    v = v.reshape(v.shape[0] // 2, 2, *v.shape[1:])
    return v[:, 0] + v[:, 1]


class Level:
    def __init__(self, refs, block, full_y, full_z, window=None):
        self.window = window
        self.u, self.g, self.cx, self.cy, self.cz, self.dg, self.inv, self.w = refs
        self.block, self.full_y, self.full_z = block, full_y, full_z
        self.shape = self.w.shape[1:]

    def from_zero(self, k_ref, lo, hi, degree, trim):
        lanes = self.shape[-1]
        zeros = jnp.zeros(self.shape, F32)
        for ref in (self.u, self.w, k_ref):
            ref[lo - 1] = zeros
            ref[hi] = zeros
        if self.full_y:
            row = lax.broadcasted_iota(jnp.int32, self.shape, 0)
        lane = lax.broadcasted_iota(jnp.int32, self.shape, len(self.shape) - 1)
        chain = [self.u, self.w] if degree % 2 else [self.w, self.u]
        targets = (self.cx, self.cy, self.cz, self.dg, self.inv, self.g, chain[0])

        def faces(planes):
            k = [k_ref[p] for p in [planes[0] - 1] + planes + [planes[-1] + 1]]
            keep = []
            for at, p in enumerate(planes):
                back, own, up = k[at:at + 3]
                ky, kyb, kz, kzb = next_row(own), last_row(own), next_lane(own), last_lane(own)
                cy = 0.5 * (own + ky)
                cz = 0.5 * (own + kz)
                if self.full_y:
                    cy = jnp.where(row == self.shape[0] - 1, 0.0, cy)
                    ky = jnp.where(row == self.shape[0] - 1, 0.0, ky)
                    kyb = jnp.where(row == 0, 0.0, kyb)
                if self.full_z:
                    cz = jnp.where(lane == lanes - 1, 0.0, cz)
                    kz = jnp.where(lane == lanes - 1, 0.0, kz)
                    kzb = jnp.where(lane == 0, 0.0, kzb)
                dg = 3.0 * own + 0.5 * ((back + up) + (ky + kyb) + (kz + kzb))
                inside = own > 0.0
                inv = jnp.where(inside, 1.0 / dg, 0.0)
                g = self.g[p] * inv
                keep.append((0.5 * (own + up), cy, cz, dg, inv, g, g * (1.0 / CENTER)))
            for p, values in zip(planes, keep):
                for ref, value in zip(targets, values):
                    ref[p] = value

        lo, hi = lo + trim, hi - trim
        self.cx[lo - 1] = 0.5 * (k_ref[lo - 1] + k_ref[lo])
        each(lo, hi, self.block, faces)
        for at, (a, b) in enumerate(cheb_weights(degree)):
            lo, hi = lo + trim, hi - trim
            self.sweep(*chain, lo, hi, a, b, at == 0)
            chain.reverse()

    def from_start(self, start, lo, hi, degree, shift):
        chain = [start, self.w]
        for a, b in [(0.0, 1.0 / CENTER)] + cheb_weights(degree):
            lo, hi = lo + 1, hi - 1
            self.sweep(*chain, lo, hi, a, b, a == 0.0, shift)
            chain.reverse()
        return chain[0]

    def sweep(self, old, new, lo, hi, a, b, first, shift=0):
        def body(planes):
            values = []
            for p, (v, z) in zip(planes, self.scaled(old, planes, shift)):
                value = (1.0 + a) * v + b * z if a else v + b * z
                values.append(value if first else value - a * new[p])
            for p, value in zip(planes, values):
                new[p] = value

        each(lo, hi, self.block, body)

    def own(self, ref, p):
        return ref[p] if self.window is None else ref[p, self.window]

    def scaled(self, u_ref, planes, shift=0):
        if self.window is not None:
            inner = lax.broadcasted_iota(jnp.int32, self.shape, 0) < self.shape[0] - 1
        u = [u_ref[p] for p in [planes[0] - 1] + planes + [planes[-1] + 1]]
        cx = [self.own(self.cx, p + shift) for p in [planes[0] - 1] + planes]
        results = []
        for at, p in enumerate(planes):
            q = p + shift
            back, v, up = u[at:at + 3]
            cy = self.own(self.cy, q)
            if self.window is not None:
                cy = jnp.where(inner, cy, 0.0)
            cz = self.own(self.cz, q)
            s = cx[at + 1] * up + cx[at] * back
            s = s + (cy * next_row(v) + last_row(cy * v))
            s = s + (cz * next_lane(v) + last_lane(cz * v))
            results.append((v, (self.own(self.g, q) + s * self.own(self.inv, q)) - v))
        return results

    def remain(self, u_ref, planes, shift=0):
        return [(v, z * self.dg[p + shift]) for p, (v, z) in zip(planes, self.scaled(u_ref, planes, shift))]


def fold_rows(ref, at, count):
    return ref[at, pl.ds(0, count, stride=2), :] + ref[at, pl.ds(1, count, stride=2), :]


def spread_rows(ref, at, value):
    count = value.shape[0]
    ref[at, pl.ds(0, count, stride=2), :] = value
    ref[at, pl.ds(1, count, stride=2), :] = value


def rows_at(i, count):
    return pl.ds(pl.multiple_of(i * count, count), count)


def by_place(reach, run):
    at = lax.axis_index("gx")
    edge = (at < reach) | (at >= lax.axis_size("gx") - reach)
    pl.when(edge)(lambda: run(0))
    pl.when(jnp.logical_not(edge))(lambda: run(1))


def take_sides(even, first, second, put):
    @pl.when(even)
    def _():
        put(1, second)
        put(17, first)

    @pl.when(jnp.logical_not(even))
    def _():
        put(1, first)
        put(17, second)


def down0(first, own, second, u, g, cx, cy, cz, dg, inv, c_out, k, w, pairs):
    def put(start, ref):
        def plane(i, carry):
            for part, to in ((0, g), (2, k)):
                to[start + i] = jnp.concatenate([rows_in(ref, part + half, i) for half in range(2)], axis=2)
            return carry

        lax.fori_loop(0, 8, plane, 0)

    put(9, own)
    take_sides(lax.axis_index("gx") % 2 == 0, first, second, put)
    level = Level((u, g, cx, cy, cz, dg, inv, w), 8, False, True)

    def keep(at, first, both):
        for half in range(2):
            rows_out(pairs, first + half, at, value=both[:, :, 128 * half:128 * half + 128])

    def fold_k(planes):
        for p in planes[::2]:
            keep((p - 1) // 2, 2, fold_tiles(k[p] + k[p + 1]))

    def fold(planes):
        r = [r for _, r in level.remain(u, planes)]
        for i in range(0, len(planes), 2):
            keep((planes[i] - 1) // 2, 0, fold_tiles(r[i] + r[i + 1]))

    def run(trim):
        level.from_zero(k, 1, 25, 3, trim)
        if trim:
            pairs[0:2] = jnp.zeros((2, 12, 24, 128), F32)
        each(1 + 4 * trim, 25 - 4 * trim, 4, fold)

    by_place(2, run)
    each(1, 25, 4, fold_k)
    half = selector(256, 128, lambda r, c: r // 2 == c)
    for part, scale in ((0, 0.5), (1, 0.125)):
        both = [pairs[2 * part + h][:, 4:20].reshape(192, 128) for h in range(2)]
        c_out[part] = (pick(jnp.concatenate(both, axis=1), half) * scale).reshape(12, 16, 128)


def down1(first, own, second, ext, u, g, cx, cy, cz, dg, inv, c_out, k, w, pairs):
    at = lax.axis_index("gx")
    count = lax.axis_size("gx")

    def put(start, ref):
        for part, to in ((0, g), (1, k)):
            to[start:start + 8] = ref[part]

    put(9, own)
    take_sides(at // 2 % 2 == 0, first, second, put)

    @pl.when(at < 2)
    def _():
        for part, to in ((0, g), (1, k)):
            to[7:9] = ext[part, 0:2]

    @pl.when(at >= count - 2)
    def _():
        for part, to in ((0, g), (1, k)):
            to[17:19] = ext[part, 2:4]

    level = Level((u, g, cx, cy, cz, dg, inv, w), 12, False, True)

    def fold_k(planes):
        for p in planes[::2]:
            pairs[1, rows_at((p - 3) // 2, 16)] = (k[p] + k[p + 1])[8:24] * 0.125

    def fold(planes):
        r = [r for _, r in level.remain(u, planes)]
        for i in range(0, len(planes), 2):
            pairs[0, rows_at((planes[i] - 3) // 2, 16)] = (r[i] + r[i + 1])[8:24] * 0.5

    def run(trim):
        level.from_zero(k, 1, 25, 3, trim)
        if trim:
            pairs[0, 0:16] = jnp.zeros((16, 128), F32)
            pairs[0, 144:160] = jnp.zeros((16, 128), F32)
        each(3 + 2 * trim, 23 - 2 * trim, 4, fold)

    by_place(3, run)
    each(3, 23, 4, fold_k)
    half = selector(256, 128, lambda r, c: r // 2 == c)
    both = jnp.concatenate([fold_rows(pairs, 0, 80), fold_rows(pairs, 1, 80)], axis=1)
    c_out[...] = pick(both, half).reshape(10, 8, 128)


def down2(low, own, high, u, g, cx, cy, cz, dg, inv, c_out, k, w, pairs):
    at = lax.axis_index("gx")
    count = lax.axis_size("gx")
    parts = own.shape[0]
    rows = 8 * parts
    lane = lax.broadcasted_iota(jnp.int32, (rows, 128), 1)

    def plane(ref, p):
        return jnp.concatenate([ref[j, p] for j in range(parts)], axis=0)

    for i in range(22):
        if i < 6:
            v = plane(low, i)
        elif i == 6:
            v = jnp.where(at < 3, plane(own, 0), plane(low, 6))
        elif i < 15:
            v = plane(own, i - 6)
        elif i == 15:
            v = jnp.where(at >= count - 3, plane(own, 9), plane(high, 0))
        else:
            v = plane(high, i - 15)
        g[i + 1] = jnp.where(lane < 64, v, 0.0)
        k[i + 1] = jnp.where(lane < 64, pltpu.roll(v, 64, 1), 0.0)
    level = Level((u, g, cx, cy, cz, dg, inv, w), 6, True, False)

    def keep(p, both, k_both):
        pairs[0, rows_at((p - 1) // 2, rows)] = jnp.where(lane < 64, both, pltpu.roll(k_both * 0.125, 64, 1))

    def fold_k(planes):
        for p in planes[::2]:
            keep(p, 0.0, k[p] + k[p + 1])

    def fold(planes):
        r = [r for _, r in level.remain(u, planes)]
        for i in range(0, len(planes), 2):
            keep(planes[i], (r[i] + r[i + 1]) * 0.5, k[planes[i]] + k[planes[i] + 1])

    def run(trim):
        level.from_zero(k, 1, 23, 3, trim)
        each(1 + 4 * trim, 23 - 4 * trim, 2, fold)
        if trim:
            each(1, 5, 4, fold_k)
            each(19, 23, 4, fold_k)

    by_place(6, run)
    half = selector(128, 128, lambda r, c: r // 2 == c)
    n = 11 * rows // 2
    both = pick(fold_rows(pairs, 0, n), half).reshape(11, rows // 2, 128)
    c_out[...] = both[:, :rows // 4] + pltpu.roll(both[:, rows // 4:], 64, 2)


def upward(first, own, second, *refs):
    at = lax.axis_index("gx")
    count = lax.axis_size("gx")
    gy = lax.axis_index("gy")
    s2, s1, s0 = refs[0:7], refs[7:14], refs[14:21]
    out, res = refs[21:23]
    s3, k3 = refs[23:31], refs[31]
    (start2, w2), (start1, w1), (start0, w0) = refs[32:34], refs[34:36], refs[36:38]
    wide2, wide1, flat0, tall = refs[38:42]
    u3, g3 = s3[0:2]
    rows3 = 2 * own.shape[1]
    rows2 = 2 * rows3
    lane = lax.broadcasted_iota(jnp.int32, (rows3, 128), 1)
    even = at // 6 % 2 == 0
    for i in range(21):
        if i < 7:
            v = jnp.where(even, second[i], first[i])
            if i >= 5:
                v = jnp.where(at < 6, own[i - 5], v)
        elif i < 14:
            v = own[i - 5]
        else:
            v = jnp.where(even, first[i - 12], second[i - 12])
            if i < 16:
                v = jnp.where(at >= count - 6, own[i - 5], v)
        v = jnp.concatenate([v, pltpu.roll(v, 64, 1)], axis=0)
        g3[i + 1] = jnp.where(lane < 32, v, 0.0)
        k3[i + 1] = jnp.where(lane < 32, pltpu.roll(v, 96, 1), 0.0)
    level = Level(s3, 7, True, False)
    level.from_zero(k3, 1, 22, 6, 1)
    spread = selector(128, 128, lambda r, c: c // 2 == r)

    fixed = []
    for p, (v, r) in zip(range(8, 15), level.remain(u3, list(range(8, 15)))):
        den = jnp.sum(level.dg[p], axis=0, keepdims=True)
        fix = jnp.sum(r, axis=0, keepdims=True) / jnp.where(den > 0.0, den, 1.0)
        fixed.append(v + jnp.where(k3[p] > 0.0, fix, 0.0))
    spread_rows(wide2, 0, pick(jnp.concatenate(fixed, axis=0), spread))
    near = pl.multiple_of(jnp.clip(8 * gy - 8, 0, rows2 - 24), 8)
    level = Level((*s2, w2), 6, True, False, pl.ds(near, 24))
    for p in range(14):
        start2[p] = level.u[p + 5, level.window] + wide2[0, pl.ds(p // 2 * rows2 + near, 24), :]
    u = level.from_start(start2, 0, 14, 3, 5)

    edge = jnp.zeros((8, 8, 128), F32)
    tall[:, 0:8, :] = edge
    tall[:, 8 + rows2:, :] = edge
    tall[:, pl.ds(pl.multiple_of(near + 8, 8), 24), :] = u[3:11]
    near = tall[:, pl.ds(pl.multiple_of(gy * 8, 8), 24), :][:, 4:20]
    spread_rows(wide1, 0, pick(near.reshape(128, 128), spread))
    level = Level((*s1, w1), 6, False, True)
    for p in range(14):
        at = (p + 1) // 2 * 32
        start1[p] = level.u[p + 6] + wide1[0, at:at + 32, :]
    u = level.from_start(start1, 0, 14, 3, 6)

    wide = jnp.concatenate([rows_in(u, i + 3, first=4, count=24) for i in range(8)], axis=0)
    wide = pick(wide.reshape(192, 128), selector(128, 256, lambda r, c: c // 2 == r)).reshape(8, 3, 8, 256)
    level = Level((*s0, w0), 7, False, True)
    for i in range(8):
        both = jnp.concatenate([wide[i, t // 2][None] for t in range(6)], axis=0)
        start0[2 * i] = level.u[2 * i + 5] + both
        start0[2 * i + 1] = level.u[2 * i + 6] + both
    u = level.from_start(start0, 0, 16, 3, 5)

    def finish(planes):
        for i, (p, values) in enumerate(zip(planes, level.remain(u, planes, 5))):
            for which, to in ((0, out), (1, res)):
                for half in range(2):
                    lanes = slice(128 * half, 128 * half + 128)
                    rows_out(flat0, which, half, i, value=values[which][:, :, lanes])
                    to[p - 4, :, lanes] = flat0[which, half, i, 8:40]

    each(4, 12, 4, finish)


def call(body, outs, scratch, name, limit):
    return pl.pallas_call(
        body,
        out_shape=[jax.ShapeDtypeStruct(shape, F32) for shape in outs],
        scratch_shapes=[pltpu.VMEM(shape, F32) for shape in scratch],
        compiler_params=pltpu.CompilerParams(vmem_limit_bytes=limit * 1024 * 1024),
        name=name,
    )


def swap(block, axis, step):
    count = lax.axis_size(axis)
    came = {}
    for side in (1, 0):
        pairs = [(t, t + step) for t in range(count - step) if t // step % 2 == side]
        came[side] = lax.ppermute(block, axis, pairs + [(b, a) for a, b in pairs])
    return came[0], came[1]


def shift(block, axis, step):
    count = lax.axis_size(axis)
    return lax.ppermute(block, axis, [(t, t + step) for t in range(count) if 0 <= t + step < count])


def shards(source, conduct):
    ny = lax.axis_size("gy")

    both = jnp.stack([array[:, :, lanes] for array in (source, conduct) for lanes in (slice(0, 128), slice(128, 256))])
    both = jnp.concatenate([shift(both[:, :, 24:], "gy", 1), both, shift(both[:, :, :8], "gy", -1)], axis=2)
    first, second = swap(both, "gx", 1)
    plane = (26, 6, 8, 256)
    *s0, c1 = call(
        down0, [plane] * 7 + [(2, 12, 16, 128)], [plane] * 2 + [(4, 12, 24, 128)], "down0", 24,
    )(first, both, second)

    c1 = jnp.concatenate([shift(c1[:, :, 8:], "gy", 1), c1, shift(c1[:, :, :8], "gy", -1)], axis=2)
    window = c1[:, 2:10]
    ext = jnp.concatenate([c1[:, 0:2], c1[:, 10:12]], axis=1)
    first, second = swap(window, "gx", 2)
    plane = (26, 32, 128)
    *s1, c2 = call(
        down1, [plane] * 7 + [(10, 8, 128)], [plane] * 2 + [(2, 160, 128)], "down1", 12,
    )(first, window, second, ext)

    c2 = lax.all_to_all(jnp.broadcast_to(c2[None], (ny, 10, 8, 128)), "gy", 0, 0)
    rows = 8 * ny
    plane = (24, rows, 128)
    *s2, c3 = call(
        down2, [plane] * 7 + [(11, rows // 4, 128)], [plane] * 2 + [(1, 11 * rows, 128)], "down2", 20,
    )(shift(c2[:, 0:7], "gx", 3), c2, shift(c2[:, 3:10], "gx", -3))

    first, second = swap(c3[1:10], "gx", 6)
    out, res = call(
        upward, [(8, 32, 256)] * 2,
        [(23, rows // 2, 128)] * 9 + [(14, 24, 128)] * 2 + [(14, 32, 128)] * 2 + [(16, 6, 8, 256)] * 2
        + [(1, 7 * rows, 128), (1, 256, 128), (2, 2, 4, 48, 128), (8, 16 + rows, 128)],
        "upward", 32,
    )(first, c3, second, *s2, *s1, *s0)
    return out, res


def solution(mesh):
    spec = P("gx", "gy", None)
    return jax.shard_map(shards, mesh=mesh, in_specs=(spec, spec), out_specs=(spec, spec), check_vma=False)
```

```python
import functools

import jax
import jax.numpy as jnp
from jax import lax
from jax.experimental import pallas as pl
from jax.experimental.pallas import tpu as pltpu
from jax.sharding import PartitionSpec as P

CENTER = 1.15
SPREAD = 0.85
RATIO = CENTER / SPREAD
F32 = jnp.float32
BF16 = jnp.bfloat16


def cheb_weights(degree):
    old = 1.0 / RATIO
    weights = []
    for _ in range(degree - 1):
        new = 1.0 / (2.0 * RATIO - old)
        weights.append((new * old, 2.0 * new / SPREAD))
        old = new
    return weights


def selector(rows, cols, test):
    r = lax.broadcasted_iota(jnp.int32, (rows, cols), 0)
    c = lax.broadcasted_iota(jnp.int32, (rows, cols), 1)
    return jnp.where(test(r, c), 1.0, 0.0).astype(BF16)


def pick(a, chosen):
    high = a.astype(BF16)
    rest = a - high.astype(F32)
    mid = rest.astype(BF16)
    low = (rest - mid.astype(F32)).astype(BF16)
    parts = [jnp.dot(part, chosen, preferred_element_type=F32) for part in (high, mid, low)]
    return parts[0] + (parts[1] + parts[2])


def each(lo, hi, block, body):
    whole = (hi - lo) // block

    def step(i, carry):
        p = lo + i * block
        body([p + b for b in range(block)])
        return carry

    if whole == 1:
        step(0, 0)
    else:
        lax.fori_loop(0, whole, step, 0)
    rest = list(range(lo + whole * block, hi))
    if rest:
        body(rest)


def next_row(v):
    if v.ndim == 2:
        return pltpu.roll(v, v.shape[0] - 1, 0)
    return jnp.concatenate([v[1:], pltpu.roll(v[:1], 7, 1)], axis=0)


def last_row(v):
    if v.ndim == 2:
        return pltpu.roll(v, 1, 0)
    return jnp.concatenate([pltpu.roll(v[-1:], 1, 1), v[:-1]], axis=0)


def next_lane(v):
    return pltpu.roll(v, v.shape[-1] - 1, v.ndim - 1)


def last_lane(v):
    return pltpu.roll(v, 1, v.ndim - 1)


def rows_in(ref, *at, first=0, count=None):
    tall = (count or ref.shape[-2]) // 8
    tiles = [ref[(*at, pl.ds(first + t, 8, stride=tall), slice(None))] for t in range(tall)]
    return jnp.concatenate([tile[None] for tile in tiles], axis=0)


def rows_out(ref, *at, value):
    for t in range(value.shape[0]):
        ref[(*at, pl.ds(t, 8, stride=value.shape[0]), slice(None))] = value[t]


def fold_tiles(v):
    v = v.reshape(v.shape[0] // 2, 2, *v.shape[1:])
    return v[:, 0] + v[:, 1]


class Level:
    def __init__(self, refs, block, full_y, full_z, window=None):
        self.window = window
        self.u, self.g, self.cx, self.cy, self.cz, self.dg, self.inv, self.w = refs
        self.block, self.full_y, self.full_z = block, full_y, full_z
        self.shape = self.w.shape[1:]

    def from_zero(self, k_ref, lo, hi, degree, trim):
        lanes = self.shape[-1]
        zeros = jnp.zeros(self.shape, F32)
        for ref in (self.u, self.w, k_ref):
            ref[lo - 1] = zeros
            ref[hi] = zeros
        if self.full_y:
            row = lax.broadcasted_iota(jnp.int32, self.shape, 0)
        lane = lax.broadcasted_iota(jnp.int32, self.shape, len(self.shape) - 1)
        chain = [self.u, self.w] if degree % 2 else [self.w, self.u]
        targets = (self.cx, self.cy, self.cz, self.dg, self.inv, self.g, chain[0])

        def faces(planes):
            k = [k_ref[p] for p in [planes[0] - 1] + planes + [planes[-1] + 1]]
            keep = []
            for at, p in enumerate(planes):
                back, own, up = k[at:at + 3]
                ky, kyb, kz, kzb = next_row(own), last_row(own), next_lane(own), last_lane(own)
                cy = 0.5 * (own + ky)
                cz = 0.5 * (own + kz)
                if self.full_y:
                    cy = jnp.where(row == self.shape[0] - 1, 0.0, cy)
                    ky = jnp.where(row == self.shape[0] - 1, 0.0, ky)
                    kyb = jnp.where(row == 0, 0.0, kyb)
                if self.full_z:
                    cz = jnp.where(lane == lanes - 1, 0.0, cz)
                    kz = jnp.where(lane == lanes - 1, 0.0, kz)
                    kzb = jnp.where(lane == 0, 0.0, kzb)
                dg = 3.0 * own + 0.5 * ((back + up) + (ky + kyb) + (kz + kzb))
                inside = own > 0.0
                inv = jnp.where(inside, 1.0 / dg, 0.0)
                g = self.g[p] * inv
                keep.append((0.5 * (own + up), cy, cz, dg, inv, g, g * (1.0 / CENTER)))
            for p, values in zip(planes, keep):
                for ref, value in zip(targets, values):
                    ref[p] = value

        lo, hi = lo + trim, hi - trim
        self.cx[lo - 1] = 0.5 * (k_ref[lo - 1] + k_ref[lo])
        each(lo, hi, self.block, faces)
        for at, (a, b) in enumerate(cheb_weights(degree)):
            lo, hi = lo + trim, hi - trim
            self.sweep(*chain, lo, hi, a, b, at == 0)
            chain.reverse()

    def from_start(self, start, lo, hi, degree, shift):
        chain = [start, self.w]
        for a, b in [(0.0, 1.0 / CENTER)] + cheb_weights(degree):
            lo, hi = lo + 1, hi - 1
            self.sweep(*chain, lo, hi, a, b, a == 0.0, shift)
            chain.reverse()
        return chain[0]

    def sweep(self, old, new, lo, hi, a, b, first, shift=0):
        def body(planes):
            values = []
            for p, (v, z) in zip(planes, self.scaled(old, planes, shift)):
                value = (1.0 + a) * v + b * z if a else v + b * z
                values.append(value if first else value - a * new[p])
            for p, value in zip(planes, values):
                new[p] = value

        each(lo, hi, self.block, body)

    def own(self, ref, p):
        return ref[p] if self.window is None else ref[p, self.window]

    def scaled(self, u_ref, planes, shift=0):
        if self.window is not None:
            inner = lax.broadcasted_iota(jnp.int32, self.shape, 0) < self.shape[0] - 1
        u = [u_ref[p] for p in [planes[0] - 1] + planes + [planes[-1] + 1]]
        cx = [self.own(self.cx, p + shift) for p in [planes[0] - 1] + planes]
        results = []
        for at, p in enumerate(planes):
            q = p + shift
            back, v, up = u[at:at + 3]
            cy = self.own(self.cy, q)
            if self.window is not None:
                cy = jnp.where(inner, cy, 0.0)
            cz = self.own(self.cz, q)
            s = cx[at + 1] * up + cx[at] * back
            s = s + (cy * next_row(v) + last_row(cy * v))
            s = s + (cz * next_lane(v) + last_lane(cz * v))
            results.append((v, (self.own(self.g, q) + s * self.own(self.inv, q)) - v))
        return results

    def remain(self, u_ref, planes, shift=0):
        return [(v, z * self.dg[p + shift]) for p, (v, z) in zip(planes, self.scaled(u_ref, planes, shift))]


def fold_rows(ref, at, count):
    return ref[at, pl.ds(0, count, stride=2), :] + ref[at, pl.ds(1, count, stride=2), :]


def spread_rows(ref, at, value):
    count = value.shape[0]
    ref[at, pl.ds(0, count, stride=2), :] = value
    ref[at, pl.ds(1, count, stride=2), :] = value


def rows_at(i, count):
    return pl.ds(pl.multiple_of(i * count, count), count)


def by_place(reach, run):
    at = lax.axis_index("gx")
    edge = (at < reach) | (at >= lax.axis_size("gx") - reach)
    pl.when(edge)(lambda: run(0))
    pl.when(jnp.logical_not(edge))(lambda: run(1))


def take_sides(even, first, second, put):
    @pl.when(even)
    def _():
        put(1, second)
        put(17, first)

    @pl.when(jnp.logical_not(even))
    def _():
        put(1, first)
        put(17, second)


def down0(first, own, second, u, g, cx, cy, cz, dg, inv, c_out, k, w, pairs):
    def put(start, ref):
        def plane(i, carry):
            for part, to in ((0, g), (2, k)):
                to[start + i] = jnp.concatenate([rows_in(ref, part + half, i) for half in range(2)], axis=2)
            return carry

        lax.fori_loop(0, 8, plane, 0)

    put(9, own)
    take_sides(lax.axis_index("gx") % 2 == 0, first, second, put)
    level = Level((u, g, cx, cy, cz, dg, inv, w), 11, False, True)

    def keep(at, first, both):
        for half in range(2):
            rows_out(pairs, first + half, at, value=both[:, :, 128 * half:128 * half + 128])

    def fold(planes):
        r = [r for _, r in level.remain(u, planes)]
        for i in range(0, len(planes), 2):
            p = planes[i]
            keep((p - 5) // 2, 0, fold_tiles(r[i] + r[i + 1]))
            keep((p - 5) // 2, 2, fold_tiles(k[p] + k[p + 1]))

    level.from_zero(k, 1, 25, 3, 1)
    each(5, 21, 8, fold)
    half = selector(256, 128, lambda r, c: r // 2 == c)
    for part, scale in ((0, 0.5), (1, 0.125)):
        both = [pairs[2 * part + h][:, 4:20].reshape(128, 128) for h in range(2)]
        c_out[part] = (pick(jnp.concatenate(both, axis=1), half) * scale).reshape(8, 16, 128)


def down1(first, own, second, u, g, cx, cy, cz, dg, inv, c_out, k, w, pairs):
    at = lax.axis_index("gx")
    count = lax.axis_size("gx")

    def put(start, ref):
        for part, to in ((0, g), (1, k)):
            to[start:start + 8] = ref[part]

    put(9, own)
    take_sides(at // 2 % 2 == 0, first, second, put)

    @pl.when(at < 2)
    def _():
        for part, to in ((0, g), (1, k)):
            to[1:7] = jnp.zeros((6, 32, 128), F32)
            to[7:9] = jnp.where(at == 1, second[part, 2:4], 0.0)

    @pl.when(at >= count - 2)
    def _():
        for part, to in ((0, g), (1, k)):
            to[17:19] = jnp.where(at == count - 2, second[part, 4:6], 0.0)
            to[19:25] = jnp.zeros((6, 32, 128), F32)

    level = Level((u, g, cx, cy, cz, dg, inv, w), 12, False, True)

    def fold_k(planes):
        for p in planes[::2]:
            pairs[1, rows_at((p - 3) // 2, 16)] = (k[p] + k[p + 1])[8:24] * 0.125

    def fold(planes):
        r = [r for _, r in level.remain(u, planes)]
        for i in range(0, len(planes), 2):
            pairs[0, rows_at((planes[i] - 3) // 2, 16)] = (r[i] + r[i + 1])[8:24] * 0.5

    def run(trim):
        level.from_zero(k, 1, 25, 3, trim)
        if trim:
            pairs[0, 0:16] = jnp.zeros((16, 128), F32)
            pairs[0, 144:160] = jnp.zeros((16, 128), F32)
        each(3 + 2 * trim, 23 - 2 * trim, 8, fold)

    by_place(3, run)
    each(3, 23, 4, fold_k)
    half = selector(256, 128, lambda r, c: r // 2 == c)
    both = jnp.concatenate([fold_rows(pairs, 0, 80), fold_rows(pairs, 1, 80)], axis=1)
    c_out[...] = pick(both, half).reshape(10, 8, 128)


def down2(low, own, high, u, g, cx, cy, cz, dg, inv, c_out, k, w, pairs):
    at = lax.axis_index("gx")
    count = lax.axis_size("gx")
    parts = own.shape[0]
    rows = 8 * parts
    lane = lax.broadcasted_iota(jnp.int32, (rows, 128), 1)

    def plane(ref, p):
        return jnp.concatenate([ref[j, p] for j in range(parts)], axis=0)

    for i in range(22):
        if i < 6:
            v = plane(low, i)
        elif i == 6:
            v = jnp.where(at < 3, plane(own, 0), plane(low, 6))
        elif i < 15:
            v = plane(own, i - 6)
        elif i == 15:
            v = jnp.where(at >= count - 3, plane(own, 9), plane(high, 0))
        else:
            v = plane(high, i - 15)
        g[i + 1] = jnp.where(lane < 64, v, 0.0)
        k[i + 1] = jnp.where(lane < 64, pltpu.roll(v, 64, 1), 0.0)
    level = Level((u, g, cx, cy, cz, dg, inv, w), 10, True, False)

    def keep(p, both, k_both):
        pairs[0, rows_at((p - 1) // 2, rows)] = jnp.where(lane < 64, both, pltpu.roll(k_both * 0.125, 64, 1))

    def fold_k(planes):
        for p in planes[::2]:
            keep(p, 0.0, k[p] + k[p + 1])

    def fold(planes):
        r = [r for _, r in level.remain(u, planes)]
        for i in range(0, len(planes), 2):
            keep(planes[i], (r[i] + r[i + 1]) * 0.5, k[planes[i]] + k[planes[i] + 1])

    def run(trim):
        level.from_zero(k, 1, 23, 3, trim)
        each(1 + 4 * trim, 23 - 4 * trim, 4, fold)
        if trim:
            each(1, 5, 4, fold_k)
            each(19, 23, 4, fold_k)

    by_place(6, run)
    half = selector(128, 128, lambda r, c: r // 2 == c)
    n = 11 * rows // 2
    both = pick(fold_rows(pairs, 0, n), half).reshape(11, rows // 2, 128)
    c_out[...] = both[:, :rows // 4] + pltpu.roll(both[:, rows // 4:], 64, 2)


def upward(first, own, second, *refs):
    at = lax.axis_index("gx")
    count = lax.axis_size("gx")
    gy = lax.axis_index("gy")
    s2, s1, s0 = refs[0:7], refs[7:14], refs[14:21]
    out, res = refs[21:23]
    s3, k3 = refs[23:31], refs[31]
    (start2, w2), (start1, w1), (start0, w0) = refs[32:34], refs[34:36], refs[36:38]
    wide2, wide1, flat0, tall = refs[38:42]
    u3, g3 = s3[0:2]
    rows3 = 2 * own.shape[1]
    rows2 = 2 * rows3
    lane = lax.broadcasted_iota(jnp.int32, (rows3, 128), 1)
    even = at // 6 % 2 == 0
    for i in range(21):
        if i < 7:
            v = jnp.where(even, second[i], first[i])
            if i >= 5:
                v = jnp.where(at < 6, own[i - 5], v)
        elif i < 14:
            v = own[i - 5]
        else:
            v = jnp.where(even, first[i - 12], second[i - 12])
            if i < 16:
                v = jnp.where(at >= count - 6, own[i - 5], v)
        v = jnp.concatenate([v, pltpu.roll(v, 64, 1)], axis=0)
        g3[i + 1] = jnp.where(lane < 32, v, 0.0)
        k3[i + 1] = jnp.where(lane < 32, pltpu.roll(v, 96, 1), 0.0)
    level = Level(s3, 7, True, False)
    level.from_zero(k3, 1, 22, 6, 1)
    spread = selector(128, 128, lambda r, c: c // 2 == r)

    fixed = []
    for p, (v, r) in zip(range(8, 15), level.remain(u3, list(range(8, 15)))):
        den = jnp.sum(level.dg[p], axis=0, keepdims=True)
        fix = jnp.sum(r, axis=0, keepdims=True) / jnp.where(den > 0.0, den, 1.0)
        fixed.append(v + jnp.where(k3[p] > 0.0, fix, 0.0))
    spread_rows(wide2, 0, pick(jnp.concatenate(fixed, axis=0), spread))
    near = pl.multiple_of(jnp.clip(8 * gy - 8, 0, rows2 - 24), 8)
    level = Level((*s2, w2), 6, True, False, pl.ds(near, 24))
    for p in range(14):
        start2[p] = level.u[p + 5, level.window] + wide2[0, pl.ds(p // 2 * rows2 + near, 24), :]
    u = level.from_start(start2, 0, 14, 3, 5)

    edge = jnp.zeros((8, 8, 128), F32)
    tall[:, 0:8, :] = edge
    tall[:, 8 + rows2:, :] = edge
    tall[:, pl.ds(pl.multiple_of(near + 8, 8), 24), :] = u[3:11]
    near = tall[:, pl.ds(pl.multiple_of(gy * 8, 8), 24), :][:, 4:20]
    spread_rows(wide1, 0, pick(near.reshape(128, 128), spread))
    level = Level((*s1, w1), 6, False, True)
    for p in range(14):
        at = (p + 1) // 2 * 32
        start1[p] = level.u[p + 6] + wide1[0, at:at + 32, :]
    u = level.from_start(start1, 0, 14, 3, 6)

    wide = jnp.concatenate([rows_in(u, i + 3, first=4, count=24) for i in range(8)], axis=0)
    wide = pick(wide.reshape(192, 128), selector(128, 256, lambda r, c: c // 2 == r)).reshape(8, 3, 8, 256)
    level = Level((*s0, w0), 7, False, True)
    for i in range(8):
        both = jnp.concatenate([wide[i, t // 2][None] for t in range(6)], axis=0)
        start0[2 * i] = level.u[2 * i + 5] + both
        start0[2 * i + 1] = level.u[2 * i + 6] + both
    u = level.from_start(start0, 0, 16, 3, 5)

    def finish(planes):
        for i, (p, values) in enumerate(zip(planes, level.remain(u, planes, 5))):
            for which, to in ((0, out), (1, res)):
                for half in range(2):
                    lanes = slice(128 * half, 128 * half + 128)
                    rows_out(flat0, which, half, i, value=values[which][:, :, lanes])
                    to[p - 4, :, lanes] = flat0[which, half, i, 8:40]

    each(4, 12, 4, finish)


def call(body, outs, scratch, name, limit):
    return pl.pallas_call(
        body,
        out_shape=[jax.ShapeDtypeStruct(shape, F32) for shape in outs],
        scratch_shapes=[pltpu.VMEM(shape, F32) for shape in scratch],
        compiler_params=pltpu.CompilerParams(vmem_limit_bytes=limit * 1024 * 1024),
        name=name,
    )


def swap(block, axis, step, ends=0):
    count = lax.axis_size(axis)
    came = {}
    for side in (1, 0):
        pairs = [(t, t + step) for t in range(count - step) if t // step % 2 == side]
        if side and ends:
            pairs += [(0, 1), (count - 2, count - 1)]
        came[side] = lax.ppermute(block, axis, pairs + [(b, a) for a, b in pairs])
    return came[0], came[1]


def shift(block, axis, step):
    count = lax.axis_size(axis)
    return lax.ppermute(block, axis, [(t, t + step) for t in range(count) if 0 <= t + step < count])


def shards(source, conduct):
    ny = lax.axis_size("gy")

    both = jnp.stack([array[:, :, lanes] for array in (source, conduct) for lanes in (slice(0, 128), slice(128, 256))])
    both = jnp.concatenate([shift(both[:, :, 24:], "gy", 1), both, shift(both[:, :, :8], "gy", -1)], axis=2)
    first, second = swap(both, "gx", 1)
    plane = (26, 6, 8, 256)
    *s0, c1 = call(
        down0, [plane] * 7 + [(2, 8, 16, 128)], [plane] * 2 + [(4, 8, 24, 128)], "down0", 24,
    )(first, both, second)

    c1 = jnp.concatenate([shift(c1[:, :, 8:], "gy", 1), c1, shift(c1[:, :, :8], "gy", -1)], axis=2)
    first, second = swap(c1, "gx", 2, 1)
    plane = (26, 32, 128)
    *s1, c2 = call(
        down1, [plane] * 7 + [(10, 8, 128)], [plane] * 2 + [(2, 160, 128)], "down1", 12,
    )(first, c1, second)

    c2 = lax.all_to_all(jnp.broadcast_to(c2[None], (ny, 10, 8, 128)), "gy", 0, 0)
    rows = 8 * ny
    plane = (24, rows, 128)
    *s2, c3 = call(
        down2, [plane] * 7 + [(11, rows // 4, 128)], [plane] * 2 + [(1, 11 * rows, 128)], "down2", 20,
    )(shift(c2[:, 0:7], "gx", 3), c2, shift(c2[:, 3:10], "gx", -3))

    first, second = swap(c3[1:10], "gx", 6)
    out, res = call(
        upward, [(8, 32, 256)] * 2,
        [(23, rows // 2, 128)] * 9 + [(14, 24, 128)] * 2 + [(14, 32, 128)] * 2 + [(16, 6, 8, 256)] * 2
        + [(1, 7 * rows, 128), (1, 256, 128), (2, 2, 4, 48, 128), (8, 16 + rows, 128)],
        "upward", 32,
    )(first, c3, second, *s2, *s1, *s0)
    return out, res


def solution(mesh):
    spec = P("gx", "gy", None)
    return jax.shard_map(shards, mesh=mesh, in_specs=(spec, spec), out_specs=(spec, spec), check_vma=False)
```

```python
import functools

import jax
import jax.numpy as jnp
from jax import lax
from jax.experimental import pallas as pl
from jax.experimental.pallas import tpu as pltpu
from jax.sharding import PartitionSpec as P

CENTER = 1.15
SPREAD = 0.85
RATIO = CENTER / SPREAD
F32 = jnp.float32
BF16 = jnp.bfloat16


def cheb_weights(degree):
    old = 1.0 / RATIO
    weights = []
    for _ in range(degree - 1):
        new = 1.0 / (2.0 * RATIO - old)
        weights.append((new * old, 2.0 * new / SPREAD))
        old = new
    return weights


def selector(rows, cols, test):
    r = lax.broadcasted_iota(jnp.int32, (rows, cols), 0)
    c = lax.broadcasted_iota(jnp.int32, (rows, cols), 1)
    return jnp.where(test(r, c), 1.0, 0.0).astype(BF16)


def pick(a, chosen):
    high = a.astype(BF16)
    rest = a - high.astype(F32)
    mid = rest.astype(BF16)
    low = (rest - mid.astype(F32)).astype(BF16)
    parts = [jnp.dot(part, chosen, preferred_element_type=F32) for part in (high, mid, low)]
    return parts[0] + (parts[1] + parts[2])


def each(lo, hi, block, body):
    whole = (hi - lo) // block

    def step(i, carry):
        p = lo + i * block
        body([p + b for b in range(block)])
        return carry

    if whole == 1:
        step(0, 0)
    elif whole:
        lax.fori_loop(0, whole, step, 0)
    rest = list(range(lo + whole * block, hi))
    if rest:
        body(rest)


def next_row(v):
    if v.ndim == 2:
        return pltpu.roll(v, v.shape[0] - 1, 0)
    return jnp.concatenate([v[1:], pltpu.roll(v[:1], 7, 1)], axis=0)


def last_row(v):
    if v.ndim == 2:
        return pltpu.roll(v, 1, 0)
    return jnp.concatenate([pltpu.roll(v[-1:], 1, 1), v[:-1]], axis=0)


def next_lane(v):
    return pltpu.roll(v, v.shape[-1] - 1, v.ndim - 1)


def last_lane(v):
    return pltpu.roll(v, 1, v.ndim - 1)


def rows_in(ref, *at, first=0, count=None):
    tall = (count or ref.shape[-2]) // 8
    tiles = [ref[(*at, pl.ds(first + t, 8, stride=tall), slice(None))] for t in range(tall)]
    return jnp.concatenate([tile[None] for tile in tiles], axis=0)


def rows_out(ref, *at, value):
    for t in range(value.shape[0]):
        ref[(*at, pl.ds(t, 8, stride=value.shape[0]), slice(None))] = value[t]


def fold_tiles(v):
    v = v.reshape(v.shape[0] // 2, 2, *v.shape[1:])
    return v[:, 0] + v[:, 1]


class Level:
    def __init__(self, refs, block, full_y, full_z, window=None):
        self.window = window
        self.u, self.g, self.cx, self.cy, self.cz, self.dg, self.inv, self.w = refs
        self.block, self.full_y, self.full_z = block, full_y, full_z
        self.shape = self.w.shape[1:]

    def from_zero(self, k_ref, lo, hi, degree, trim):
        lanes = self.shape[-1]
        zeros = jnp.zeros(self.shape, F32)
        for ref in (self.u, self.w, k_ref):
            ref[lo - 1] = zeros
            ref[hi] = zeros
        if self.full_y:
            row = lax.broadcasted_iota(jnp.int32, self.shape, 0)
        lane = lax.broadcasted_iota(jnp.int32, self.shape, len(self.shape) - 1)
        chain = [self.u, self.w] if degree % 2 else [self.w, self.u]
        targets = (self.cx, self.cy, self.cz, self.dg, self.inv, self.g, chain[0])

        def faces(planes):
            k = [k_ref[p] for p in [planes[0] - 1] + planes + [planes[-1] + 1]]
            keep = []
            for at, p in enumerate(planes):
                back, own, up = k[at:at + 3]
                ky, kyb, kz, kzb = next_row(own), last_row(own), next_lane(own), last_lane(own)
                cy = 0.5 * (own + ky)
                cz = 0.5 * (own + kz)
                if self.full_y:
                    cy = jnp.where(row == self.shape[0] - 1, 0.0, cy)
                    ky = jnp.where(row == self.shape[0] - 1, 0.0, ky)
                    kyb = jnp.where(row == 0, 0.0, kyb)
                if self.full_z:
                    cz = jnp.where(lane == lanes - 1, 0.0, cz)
                    kz = jnp.where(lane == lanes - 1, 0.0, kz)
                    kzb = jnp.where(lane == 0, 0.0, kzb)
                dg = 3.0 * own + 0.5 * ((back + up) + (ky + kyb) + (kz + kzb))
                inside = own > 0.0
                inv = jnp.where(inside, 1.0 / dg, 0.0)
                g = self.g[p] * inv
                keep.append((0.5 * (own + up), cy, cz, dg, inv, g, g * (1.0 / CENTER)))
            for p, values in zip(planes, keep):
                for ref, value in zip(targets, values):
                    ref[p] = value

        lo, hi = lo + trim, hi - trim
        self.cx[lo - 1] = 0.5 * (k_ref[lo - 1] + k_ref[lo])
        each(lo, hi, self.block, faces)
        for at, (a, b) in enumerate(cheb_weights(degree)):
            lo, hi = lo + trim, hi - trim
            self.sweep(*chain, lo, hi, a, b, at == 0)
            chain.reverse()

    def from_start(self, start, lo, hi, degree, shift):
        chain = [start, self.w]
        for a, b in [(0.0, 1.0 / CENTER)] + cheb_weights(degree):
            lo, hi = lo + 1, hi - 1
            self.sweep(*chain, lo, hi, a, b, a == 0.0, shift)
            chain.reverse()
        return chain[0]

    def sweep(self, old, new, lo, hi, a, b, first, shift=0):
        def body(planes):
            values = []
            for p, (v, z) in zip(planes, self.scaled(old, planes, shift)):
                value = (1.0 + a) * v + b * z if a else v + b * z
                values.append(value if first else value - a * new[p])
            for p, value in zip(planes, values):
                new[p] = value

        each(lo, hi, self.block, body)

    def own(self, ref, p):
        return ref[p] if self.window is None else ref[p, self.window]

    def scaled(self, u_ref, planes, shift=0):
        if self.window is not None:
            inner = lax.broadcasted_iota(jnp.int32, self.shape, 0) < self.shape[0] - 1
        u = [u_ref[p] for p in [planes[0] - 1] + planes + [planes[-1] + 1]]
        cx = [self.own(self.cx, p + shift) for p in [planes[0] - 1] + planes]
        results = []
        for at, p in enumerate(planes):
            q = p + shift
            back, v, up = u[at:at + 3]
            cy = self.own(self.cy, q)
            if self.window is not None:
                cy = jnp.where(inner, cy, 0.0)
            cz = self.own(self.cz, q)
            s = cx[at + 1] * up + cx[at] * back
            s = s + (cy * next_row(v) + last_row(cy * v))
            s = s + (cz * next_lane(v) + last_lane(cz * v))
            results.append((v, (self.own(self.g, q) + s * self.own(self.inv, q)) - v))
        return results

    def remain(self, u_ref, planes, shift=0):
        return [(v, z * self.dg[p + shift]) for p, (v, z) in zip(planes, self.scaled(u_ref, planes, shift))]


def fold_rows(ref, at, count):
    return ref[at, pl.ds(0, count, stride=2), :] + ref[at, pl.ds(1, count, stride=2), :]


def spread_rows(ref, at, value):
    count = value.shape[0]
    ref[at, pl.ds(0, count, stride=2), :] = value
    ref[at, pl.ds(1, count, stride=2), :] = value


def rows_at(i, count):
    return pl.ds(pl.multiple_of(i * count, count), count)


def by_place(reach, run):
    at = lax.axis_index("gx")
    edge = (at < reach) | (at >= lax.axis_size("gx") - reach)
    pl.when(edge)(lambda: run(0))
    pl.when(jnp.logical_not(edge))(lambda: run(1))


def take_sides(even, first, second, put):
    @pl.when(even)
    def _():
        put(1, second)
        put(17, first)

    @pl.when(jnp.logical_not(even))
    def _():
        put(1, first)
        put(17, second)


def down0(first, own, second, u, g, cx, cy, cz, dg, inv, c_out, k, w, pairs):
    def put(start, ref):
        def plane(i, carry):
            for part, to in ((0, g), (2, k)):
                to[start + i] = jnp.concatenate([rows_in(ref, part + half, i) for half in range(2)], axis=2)
            return carry

        lax.fori_loop(0, 8, plane, 0)

    put(9, own)
    take_sides(lax.axis_index("gx") % 2 == 0, first, second, put)
    level = Level((u, g, cx, cy, cz, dg, inv, w), 11, False, True)

    def keep(at, first, both):
        for half in range(2):
            rows_out(pairs, first + half, at, value=both[:, :, 128 * half:128 * half + 128])

    def fold(planes):
        r = [r for _, r in level.remain(u, planes)]
        for i in range(0, len(planes), 2):
            p = planes[i]
            keep((p - 5) // 2, 0, fold_tiles(r[i] + r[i + 1]))
            keep((p - 5) // 2, 2, fold_tiles(k[p] + k[p + 1]))

    level.from_zero(k, 1, 25, 3, 1)
    each(5, 21, 8, fold)
    half = selector(256, 128, lambda r, c: r // 2 == c)
    for part, scale in ((0, 0.5), (1, 0.125)):
        both = [pairs[2 * part + h][:, 4:20].reshape(128, 128) for h in range(2)]
        c_out[part] = (pick(jnp.concatenate(both, axis=1), half) * scale).reshape(8, 16, 128)


def down1(first, own, second, u, g, cx, cy, cz, dg, inv, c_out, k, w, pairs):
    at = lax.axis_index("gx")
    count = lax.axis_size("gx")

    def put(start, ref):
        for part, to in ((0, g), (1, k)):
            to[start:start + 8] = ref[part]

    put(9, own)
    take_sides(at // 2 % 2 == 0, first, second, put)

    @pl.when(at < 2)
    def _():
        for part, to in ((0, g), (1, k)):
            to[1:7] = jnp.zeros((6, 32, 128), F32)
            to[7:9] = jnp.where(at == 1, second[part, 2:4], 0.0)

    @pl.when(at >= count - 2)
    def _():
        for part, to in ((0, g), (1, k)):
            to[17:19] = jnp.where(at == count - 2, second[part, 4:6], 0.0)
            to[19:25] = jnp.zeros((6, 32, 128), F32)

    level = Level((u, g, cx, cy, cz, dg, inv, w), 24, False, True)

    def fold_k(planes):
        for p in planes[::2]:
            pairs[1, rows_at((p - 3) // 2, 16)] = (k[p] + k[p + 1])[8:24] * 0.125

    def fold(planes):
        r = [r for _, r in level.remain(u, planes)]
        for i in range(0, len(planes), 2):
            pairs[0, rows_at((planes[i] - 3) // 2, 16)] = (r[i] + r[i + 1])[8:24] * 0.5

    def run(trim):
        level.from_zero(k, 1, 25, 3, trim)
        if trim:
            pairs[0, 0:16] = jnp.zeros((16, 128), F32)
            pairs[0, 144:160] = jnp.zeros((16, 128), F32)
        each(3 + 2 * trim, 23 - 2 * trim, 20, fold)

    by_place(3, run)
    each(3, 23, 4, fold_k)
    half = selector(256, 128, lambda r, c: r // 2 == c)
    both = jnp.concatenate([fold_rows(pairs, 0, 80), fold_rows(pairs, 1, 80)], axis=1)
    c_out[...] = pick(both, half).reshape(10, 8, 128)


def down2(low, own, high, u, g, cx, cy, cz, dg, inv, c_out, k, w, pairs):
    at = lax.axis_index("gx")
    count = lax.axis_size("gx")
    parts = own.shape[0]
    rows = 8 * parts
    lane = lax.broadcasted_iota(jnp.int32, (rows, 128), 1)

    def plane(ref, p):
        return jnp.concatenate([ref[j, p] for j in range(parts)], axis=0)

    for i in range(22):
        if i < 6:
            v = plane(low, i)
        elif i == 6:
            v = jnp.where(at < 3, plane(own, 0), plane(low, 6))
        elif i < 15:
            v = plane(own, i - 6)
        elif i == 15:
            v = jnp.where(at >= count - 3, plane(own, 9), plane(high, 0))
        else:
            v = plane(high, i - 15)
        g[i + 1] = jnp.where(lane < 64, v, 0.0)
        k[i + 1] = jnp.where(lane < 64, pltpu.roll(v, 64, 1), 0.0)
    level = Level((u, g, cx, cy, cz, dg, inv, w), 20, True, False)

    def keep(p, both, k_both):
        pairs[0, rows_at((p - 1) // 2, rows)] = jnp.where(lane < 64, both, pltpu.roll(k_both * 0.125, 64, 1))

    def fold_k(planes):
        for p in planes[::2]:
            keep(p, 0.0, k[p] + k[p + 1])

    def fold(planes):
        r = [r for _, r in level.remain(u, planes)]
        for i in range(0, len(planes), 2):
            keep(planes[i], (r[i] + r[i + 1]) * 0.5, k[planes[i]] + k[planes[i] + 1])

    def run(trim):
        level.from_zero(k, 1, 23, 3, trim)
        each(1 + 4 * trim, 23 - 4 * trim, 4, fold)
        if trim:
            each(1, 5, 4, fold_k)
            each(19, 23, 4, fold_k)

    by_place(6, run)
    half = selector(128, 128, lambda r, c: r // 2 == c)
    n = 11 * rows // 2
    both = pick(fold_rows(pairs, 0, n), half).reshape(11, rows // 2, 128)
    c_out[...] = both[:, :rows // 4] + pltpu.roll(both[:, rows // 4:], 64, 2)


def upward(first, own, second, *refs):
    at = lax.axis_index("gx")
    count = lax.axis_size("gx")
    gy = lax.axis_index("gy")
    s2, s1, s0 = refs[0:7], refs[7:14], refs[14:21]
    out, res = refs[21:23]
    s3, k3 = refs[23:31], refs[31]
    (start2, w2), (start1, w1), (start0, w0) = refs[32:34], refs[34:36], refs[36:38]
    wide2, wide1, flat0, tall = refs[38:42]
    u3, g3 = s3[0:2]
    rows3 = 2 * own.shape[1]
    rows2 = 2 * rows3
    lane = lax.broadcasted_iota(jnp.int32, (rows3, 128), 1)
    even = at // 6 % 2 == 0
    for i in range(21):
        if i < 7:
            v = jnp.where(even, second[i], first[i])
            if i >= 5:
                v = jnp.where(at < 6, own[i - 5], v)
        elif i < 14:
            v = own[i - 5]
        else:
            v = jnp.where(even, first[i - 12], second[i - 12])
            if i < 16:
                v = jnp.where(at >= count - 6, own[i - 5], v)
        v = jnp.concatenate([v, pltpu.roll(v, 64, 1)], axis=0)
        g3[i + 1] = jnp.where(lane < 32, v, 0.0)
        k3[i + 1] = jnp.where(lane < 32, pltpu.roll(v, 96, 1), 0.0)
    level = Level(s3, 20, True, False)
    level.from_zero(k3, 1, 22, 6, 1)
    spread = selector(128, 128, lambda r, c: c // 2 == r)

    fixed = []
    for p, (v, r) in zip(range(8, 15), level.remain(u3, list(range(8, 15)))):
        den = jnp.sum(level.dg[p], axis=0, keepdims=True)
        fix = jnp.sum(r, axis=0, keepdims=True) / jnp.where(den > 0.0, den, 1.0)
        fixed.append(v + jnp.where(k3[p] > 0.0, fix, 0.0))
    spread_rows(wide2, 0, pick(jnp.concatenate(fixed, axis=0), spread))
    near = pl.multiple_of(jnp.clip(8 * gy - 8, 0, rows2 - 24), 8)
    level = Level((*s2, w2), 12, True, False, pl.ds(near, 24))
    for p in range(14):
        start2[p] = level.u[p + 5, level.window] + wide2[0, pl.ds(p // 2 * rows2 + near, 24), :]
    u = level.from_start(start2, 0, 14, 3, 5)

    edge = jnp.zeros((8, 8, 128), F32)
    tall[:, 0:8, :] = edge
    tall[:, 8 + rows2:, :] = edge
    tall[:, pl.ds(pl.multiple_of(near + 8, 8), 24), :] = u[3:11]
    near = tall[:, pl.ds(pl.multiple_of(gy * 8, 8), 24), :][:, 4:20]
    spread_rows(wide1, 0, pick(near.reshape(128, 128), spread))
    level = Level((*s1, w1), 12, False, True)
    for p in range(14):
        at = (p + 1) // 2 * 32
        start1[p] = level.u[p + 6] + wide1[0, at:at + 32, :]
    u = level.from_start(start1, 0, 14, 3, 6)

    wide = jnp.concatenate([rows_in(u, i + 3, first=4, count=24) for i in range(8)], axis=0)
    wide = pick(wide.reshape(192, 128), selector(128, 256, lambda r, c: c // 2 == r)).reshape(8, 3, 8, 256)
    level = Level((*s0, w0), 14, False, True)
    for i in range(8):
        both = jnp.concatenate([wide[i, t // 2][None] for t in range(6)], axis=0)
        start0[2 * i] = level.u[2 * i + 5] + both
        start0[2 * i + 1] = level.u[2 * i + 6] + both
    u = level.from_start(start0, 0, 16, 3, 5)

    def finish(planes):
        for i, (p, values) in enumerate(zip(planes, level.remain(u, planes, 5))):
            for which, to in ((0, out), (1, res)):
                for half in range(2):
                    lanes = slice(128 * half, 128 * half + 128)
                    rows_out(flat0, which, half, i, value=values[which][:, :, lanes])
                    to[p - 4, :, lanes] = flat0[which, half, i, 8:40]

    each(4, 12, 8, finish)


def call(body, outs, scratch, name, limit):
    return pl.pallas_call(
        body,
        out_shape=[jax.ShapeDtypeStruct(shape, F32) for shape in outs],
        scratch_shapes=[pltpu.VMEM(shape, F32) for shape in scratch],
        compiler_params=pltpu.CompilerParams(vmem_limit_bytes=limit * 1024 * 1024),
        name=name,
    )


def swap(block, axis, step, ends=0):
    count = lax.axis_size(axis)
    came = {}
    for side in (1, 0):
        pairs = [(t, t + step) for t in range(count - step) if t // step % 2 == side]
        if side and ends:
            pairs += [(0, 1), (count - 2, count - 1)]
        came[side] = lax.ppermute(block, axis, pairs + [(b, a) for a, b in pairs])
    return came[0], came[1]


def shift(block, axis, step):
    count = lax.axis_size(axis)
    return lax.ppermute(block, axis, [(t, t + step) for t in range(count) if 0 <= t + step < count])


def shards(source, conduct):
    ny = lax.axis_size("gy")

    both = jnp.stack([array[:, :, lanes] for array in (source, conduct) for lanes in (slice(0, 128), slice(128, 256))])
    both = jnp.concatenate([shift(both[:, :, 24:], "gy", 1), both, shift(both[:, :, :8], "gy", -1)], axis=2)
    first, second = swap(both, "gx", 1)
    plane = (26, 6, 8, 256)
    *s0, c1 = call(
        down0, [plane] * 7 + [(2, 8, 16, 128)], [plane] * 2 + [(4, 8, 24, 128)], "down0", 24,
    )(first, both, second)

    c1 = jnp.concatenate([shift(c1[:, :, 8:], "gy", 1), c1, shift(c1[:, :, :8], "gy", -1)], axis=2)
    first, second = swap(c1, "gx", 2, 1)
    plane = (26, 32, 128)
    *s1, c2 = call(
        down1, [plane] * 7 + [(10, 8, 128)], [plane] * 2 + [(2, 160, 128)], "down1", 12,
    )(first, c1, second)

    c2 = lax.all_to_all(jnp.broadcast_to(c2[None], (ny, 10, 8, 128)), "gy", 0, 0)
    rows = 8 * ny
    plane = (24, rows, 128)
    *s2, c3 = call(
        down2, [plane] * 7 + [(11, rows // 4, 128)], [plane] * 2 + [(1, 11 * rows, 128)], "down2", 20,
    )(shift(c2[:, 0:7], "gx", 3), c2, shift(c2[:, 3:10], "gx", -3))

    first, second = swap(c3[1:10], "gx", 6)
    out, res = call(
        upward, [(8, 32, 256)] * 2,
        [(23, rows // 2, 128)] * 9 + [(14, 24, 128)] * 2 + [(14, 32, 128)] * 2 + [(16, 6, 8, 256)] * 2
        + [(1, 7 * rows, 128), (1, 256, 128), (2, 2, 8, 48, 128), (8, 16 + rows, 128)],
        "upward", 32,
    )(first, c3, second, *s2, *s1, *s0)
    return out, res


def solution(mesh):
    spec = P("gx", "gy", None)
    return jax.shard_map(shards, mesh=mesh, in_specs=(spec, spec), out_specs=(spec, spec), check_vma=False)
```

```python
import functools

import jax
import jax.numpy as jnp
from jax import lax
from jax.experimental import pallas as pl
from jax.experimental.pallas import tpu as pltpu
from jax.sharding import PartitionSpec as P

CENTER = 1.15
SPREAD = 0.85
RATIO = CENTER / SPREAD
F32 = jnp.float32
BF16 = jnp.bfloat16


def cheb_weights(degree):
    old = 1.0 / RATIO
    weights = []
    for _ in range(degree - 1):
        new = 1.0 / (2.0 * RATIO - old)
        weights.append((new * old, 2.0 * new / SPREAD))
        old = new
    return weights


def selector(rows, cols, test):
    r = lax.broadcasted_iota(jnp.int32, (rows, cols), 0)
    c = lax.broadcasted_iota(jnp.int32, (rows, cols), 1)
    return jnp.where(test(r, c), 1.0, 0.0).astype(BF16)


def pick(a, chosen):
    high = a.astype(BF16)
    rest = a - high.astype(F32)
    mid = rest.astype(BF16)
    low = (rest - mid.astype(F32)).astype(BF16)
    parts = [jnp.dot(part, chosen, preferred_element_type=F32) for part in (high, mid, low)]
    return parts[0] + (parts[1] + parts[2])


def each(lo, hi, block, body):
    whole = (hi - lo) // block

    def step(i, carry):
        p = lo + i * block
        body([p + b for b in range(block)])
        return carry

    if whole == 1:
        step(0, 0)
    elif whole:
        lax.fori_loop(0, whole, step, 0)
    rest = list(range(lo + whole * block, hi))
    if rest:
        body(rest)


def next_row(v):
    if v.ndim == 2:
        return pltpu.roll(v, v.shape[0] - 1, 0)
    return jnp.concatenate([v[1:], pltpu.roll(v[:1], 7, 1)], axis=0)


def last_row(v):
    if v.ndim == 2:
        return pltpu.roll(v, 1, 0)
    return jnp.concatenate([pltpu.roll(v[-1:], 1, 1), v[:-1]], axis=0)


def next_lane(v):
    return pltpu.roll(v, v.shape[-1] - 1, v.ndim - 1)


def last_lane(v):
    return pltpu.roll(v, 1, v.ndim - 1)


def rows_in(ref, *at, first=0, count=None):
    tall = (count or ref.shape[-2]) // 8
    tiles = [ref[(*at, pl.ds(first + t, 8, stride=tall), slice(None))] for t in range(tall)]
    return jnp.concatenate([tile[None] for tile in tiles], axis=0)


def rows_out(ref, *at, value):
    for t in range(value.shape[0]):
        ref[(*at, pl.ds(t, 8, stride=value.shape[0]), slice(None))] = value[t]


def fold_tiles(v):
    v = v.reshape(v.shape[0] // 2, 2, *v.shape[1:])
    return v[:, 0] + v[:, 1]


class Level:
    def __init__(self, refs, block, full_y, full_z, window=None):
        self.window = window
        self.u, self.g, self.cx, self.cy, self.cz, self.dg, self.inv, self.w = refs
        self.block, self.full_y, self.full_z = block, full_y, full_z
        self.shape = self.w.shape[1:]

    def from_zero(self, k_ref, lo, hi, degree, trim):
        lanes = self.shape[-1]
        zeros = jnp.zeros(self.shape, F32)
        for ref in (self.u, self.w, k_ref):
            ref[lo - 1] = zeros
            ref[hi] = zeros
        if self.full_y:
            row = lax.broadcasted_iota(jnp.int32, self.shape, 0)
        lane = lax.broadcasted_iota(jnp.int32, self.shape, len(self.shape) - 1)
        chain = [self.u, self.w] if degree % 2 else [self.w, self.u]
        targets = (self.cx, self.cy, self.cz, self.dg, self.inv, self.g, chain[0])

        def faces(planes):
            k = [k_ref[p] for p in [planes[0] - 1] + planes + [planes[-1] + 1]]
            keep = []
            for at, p in enumerate(planes):
                back, own, up = k[at:at + 3]
                ky, kyb, kz, kzb = next_row(own), last_row(own), next_lane(own), last_lane(own)
                cy = 0.5 * (own + ky)
                cz = 0.5 * (own + kz)
                if self.full_y:
                    cy = jnp.where(row == self.shape[0] - 1, 0.0, cy)
                    ky = jnp.where(row == self.shape[0] - 1, 0.0, ky)
                    kyb = jnp.where(row == 0, 0.0, kyb)
                if self.full_z:
                    cz = jnp.where(lane == lanes - 1, 0.0, cz)
                    kz = jnp.where(lane == lanes - 1, 0.0, kz)
                    kzb = jnp.where(lane == 0, 0.0, kzb)
                dg = 3.0 * own + 0.5 * ((back + up) + (ky + kyb) + (kz + kzb))
                inside = own > 0.0
                inv = jnp.where(inside, 1.0 / dg, 0.0)
                g = self.g[p] * inv
                keep.append((0.5 * (own + up), cy, cz, dg, inv, g, g * (1.0 / CENTER)))
            for p, values in zip(planes, keep):
                for ref, value in zip(targets, values):
                    ref[p] = value

        lo, hi = lo + trim, hi - trim
        self.cx[lo - 1] = 0.5 * (k_ref[lo - 1] + k_ref[lo])
        each(lo, hi, self.block, faces)
        for at, (a, b) in enumerate(cheb_weights(degree)):
            lo, hi = lo + trim, hi - trim
            self.sweep(*chain, lo, hi, a, b, at == 0)
            chain.reverse()

    def from_start(self, start, lo, hi, degree, shift):
        chain = [start, self.w]
        for a, b in [(0.0, 1.0 / CENTER)] + cheb_weights(degree):
            lo, hi = lo + 1, hi - 1
            self.sweep(*chain, lo, hi, a, b, a == 0.0, shift)
            chain.reverse()
        return chain[0]

    def sweep(self, old, new, lo, hi, a, b, first, shift=0):
        def body(planes):
            values = []
            for p, (v, z) in zip(planes, self.scaled(old, planes, shift)):
                value = (1.0 + a) * v + b * z if a else v + b * z
                values.append(value if first else value - a * new[p])
            for p, value in zip(planes, values):
                new[p] = value

        each(lo, hi, self.block, body)

    def own(self, ref, p):
        return ref[p] if self.window is None else ref[p, self.window]

    def scaled(self, u_ref, planes, shift=0):
        if self.window is not None:
            inner = lax.broadcasted_iota(jnp.int32, self.shape, 0) < self.shape[0] - 1
        u = [u_ref[p] for p in [planes[0] - 1] + planes + [planes[-1] + 1]]
        cx = [self.own(self.cx, p + shift) for p in [planes[0] - 1] + planes]
        results = []
        for at, p in enumerate(planes):
            q = p + shift
            back, v, up = u[at:at + 3]
            cy = self.own(self.cy, q)
            if self.window is not None:
                cy = jnp.where(inner, cy, 0.0)
            cz = self.own(self.cz, q)
            s = cx[at + 1] * up + cx[at] * back
            s = s + (cy * next_row(v) + last_row(cy * v))
            s = s + (cz * next_lane(v) + last_lane(cz * v))
            results.append((v, (self.own(self.g, q) + s * self.own(self.inv, q)) - v))
        return results

    def remain(self, u_ref, planes, shift=0):
        return [(v, z * self.dg[p + shift]) for p, (v, z) in zip(planes, self.scaled(u_ref, planes, shift))]


def fold_rows(ref, at, count):
    return ref[at, pl.ds(0, count, stride=2), :] + ref[at, pl.ds(1, count, stride=2), :]


def spread_rows(ref, at, value):
    count = value.shape[0]
    ref[at, pl.ds(0, count, stride=2), :] = value
    ref[at, pl.ds(1, count, stride=2), :] = value


def rows_at(i, count):
    return pl.ds(pl.multiple_of(i * count, count), count)


def by_place(reach, run):
    at = lax.axis_index("gx")
    edge = (at < reach) | (at >= lax.axis_size("gx") - reach)
    pl.when(edge)(lambda: run(0))
    pl.when(jnp.logical_not(edge))(lambda: run(1))


def take_sides(even, first, second, put):
    @pl.when(even)
    def _():
        put(1, second)
        put(17, first)

    @pl.when(jnp.logical_not(even))
    def _():
        put(1, first)
        put(17, second)


def down0(first, own, second, u, g, cx, cy, cz, dg, inv, c_out, k, w, pairs):
    def put(start, ref):
        def plane(i, carry):
            for part, to in ((0, g), (2, k)):
                to[start + i] = jnp.concatenate([rows_in(ref, part + half, i) for half in range(2)], axis=2)
            return carry

        lax.fori_loop(0, 8, plane, 0)

    put(9, own)
    take_sides(lax.axis_index("gx") % 2 == 0, first, second, put)
    level = Level((u, g, cx, cy, cz, dg, inv, w), 22, False, True)

    def keep(at, first, both):
        for half in range(2):
            rows_out(pairs, first + half, at, value=both[:, :, 128 * half:128 * half + 128])

    def fold(planes):
        r = [r for _, r in level.remain(u, planes)]
        for i in range(0, len(planes), 2):
            p = planes[i]
            keep((p - 5) // 2, 0, fold_tiles(r[i] + r[i + 1]))
            keep((p - 5) // 2, 2, fold_tiles(k[p] + k[p + 1]))

    level.from_zero(k, 1, 25, 3, 1)
    each(5, 21, 16, fold)
    half = selector(256, 128, lambda r, c: r // 2 == c)
    for part, scale in ((0, 0.5), (1, 0.125)):
        both = [pairs[2 * part + h][:, 4:20].reshape(128, 128) for h in range(2)]
        c_out[part] = (pick(jnp.concatenate(both, axis=1), half) * scale).reshape(8, 16, 128)


def down1(first, own, second, u, g, cx, cy, cz, dg, inv, c_out, k, w, pairs):
    at = lax.axis_index("gx")
    count = lax.axis_size("gx")

    def put(start, ref):
        for part, to in ((0, g), (1, k)):
            to[start:start + 8] = ref[part]

    put(9, own)
    take_sides(at // 2 % 2 == 0, first, second, put)

    @pl.when(at < 2)
    def _():
        for part, to in ((0, g), (1, k)):
            to[1:7] = jnp.zeros((6, 32, 128), F32)
            to[7:9] = jnp.where(at == 1, second[part, 2:4], 0.0)

    @pl.when(at >= count - 2)
    def _():
        for part, to in ((0, g), (1, k)):
            to[17:19] = jnp.where(at == count - 2, second[part, 4:6], 0.0)
            to[19:25] = jnp.zeros((6, 32, 128), F32)

    level = Level((u, g, cx, cy, cz, dg, inv, w), 24, False, True)

    def fold_k(planes):
        for p in planes[::2]:
            pairs[1, rows_at((p - 3) // 2, 16)] = (k[p] + k[p + 1])[8:24] * 0.125

    def fold(planes):
        r = [r for _, r in level.remain(u, planes)]
        for i in range(0, len(planes), 2):
            pairs[0, rows_at((planes[i] - 3) // 2, 16)] = (r[i] + r[i + 1])[8:24] * 0.5

    def run(trim):
        level.from_zero(k, 1, 25, 3, trim)
        if trim:
            pairs[0, 0:16] = jnp.zeros((16, 128), F32)
            pairs[0, 144:160] = jnp.zeros((16, 128), F32)
        each(3 + 2 * trim, 23 - 2 * trim, 20, fold)

    by_place(3, run)
    each(3, 23, 4, fold_k)
    half = selector(256, 128, lambda r, c: r // 2 == c)
    both = jnp.concatenate([fold_rows(pairs, 0, 80), fold_rows(pairs, 1, 80)], axis=1)
    c_out[...] = pick(both, half).reshape(10, 8, 128)


def down2(low, own, high, u, g, cx, cy, cz, dg, inv, c_out, k, w, pairs):
    at = lax.axis_index("gx")
    count = lax.axis_size("gx")
    parts = own.shape[0]
    rows = 8 * parts
    lane = lax.broadcasted_iota(jnp.int32, (rows, 128), 1)

    def plane(ref, p):
        return jnp.concatenate([ref[j, p] for j in range(parts)], axis=0)

    for i in range(22):
        if i < 6:
            v = plane(low, i)
        elif i == 6:
            v = jnp.where(at < 3, plane(own, 0), plane(low, 6))
        elif i < 15:
            v = plane(own, i - 6)
        elif i == 15:
            v = jnp.where(at >= count - 3, plane(own, 9), plane(high, 0))
        else:
            v = plane(high, i - 15)
        g[i + 1] = jnp.where(lane < 64, v, 0.0)
        k[i + 1] = jnp.where(lane < 64, pltpu.roll(v, 64, 1), 0.0)
    level = Level((u, g, cx, cy, cz, dg, inv, w), 20, True, False)

    def keep(p, both, k_both):
        pairs[0, rows_at((p - 1) // 2, rows)] = jnp.where(lane < 64, both, pltpu.roll(k_both * 0.125, 64, 1))

    def fold_k(planes):
        for p in planes[::2]:
            keep(p, 0.0, k[p] + k[p + 1])

    def fold(planes):
        r = [r for _, r in level.remain(u, planes)]
        for i in range(0, len(planes), 2):
            keep(planes[i], (r[i] + r[i + 1]) * 0.5, k[planes[i]] + k[planes[i] + 1])

    def run(trim):
        level.from_zero(k, 1, 23, 3, trim)
        each(1 + 4 * trim, 23 - 4 * trim, 14, fold)
        if trim:
            each(1, 5, 4, fold_k)
            each(19, 23, 4, fold_k)

    by_place(6, run)
    half = selector(128, 128, lambda r, c: r // 2 == c)
    n = 11 * rows // 2
    both = pick(fold_rows(pairs, 0, n), half).reshape(11, rows // 2, 128)
    c_out[...] = both[:, :rows // 4] + pltpu.roll(both[:, rows // 4:], 64, 2)


def upward(first, own, second, *refs):
    at = lax.axis_index("gx")
    count = lax.axis_size("gx")
    gy = lax.axis_index("gy")
    s2, s1, s0 = refs[0:7], refs[7:14], refs[14:21]
    out, res = refs[21:23]
    s3, k3 = refs[23:31], refs[31]
    (start2, w2), (start1, w1), (start0, w0) = refs[32:34], refs[34:36], refs[36:38]
    wide2, wide1, flat0, tall, done, sems = refs[38:44]
    u3, g3 = s3[0:2]
    rows3 = 2 * own.shape[1]
    rows2 = 2 * rows3
    lane = lax.broadcasted_iota(jnp.int32, (rows3, 128), 1)
    even = at // 6 % 2 == 0
    for i in range(21):
        if i < 7:
            v = jnp.where(even, second[i], first[i])
            if i >= 5:
                v = jnp.where(at < 6, own[i - 5], v)
        elif i < 14:
            v = own[i - 5]
        else:
            v = jnp.where(even, first[i - 12], second[i - 12])
            if i < 16:
                v = jnp.where(at >= count - 6, own[i - 5], v)
        v = jnp.concatenate([v, pltpu.roll(v, 64, 1)], axis=0)
        g3[i + 1] = jnp.where(lane < 32, v, 0.0)
        k3[i + 1] = jnp.where(lane < 32, pltpu.roll(v, 96, 1), 0.0)
    level = Level(s3, 20, True, False)
    level.from_zero(k3, 1, 22, 6, 1)
    spread = selector(128, 128, lambda r, c: c // 2 == r)

    fixed = []
    for p, (v, r) in zip(range(8, 15), level.remain(u3, list(range(8, 15)))):
        den = jnp.sum(level.dg[p], axis=0, keepdims=True)
        fix = jnp.sum(r, axis=0, keepdims=True) / jnp.where(den > 0.0, den, 1.0)
        fixed.append(v + jnp.where(k3[p] > 0.0, fix, 0.0))
    spread_rows(wide2, 0, pick(jnp.concatenate(fixed, axis=0), spread))
    near = pl.multiple_of(jnp.clip(8 * gy - 8, 0, rows2 - 24), 8)
    level = Level((*s2, w2), 12, True, False, pl.ds(near, 24))
    for p in range(14):
        start2[p] = level.u[p + 5, level.window] + wide2[0, pl.ds(p // 2 * rows2 + near, 24), :]
    u = level.from_start(start2, 0, 14, 3, 5)

    edge = jnp.zeros((8, 8, 128), F32)
    tall[:, 0:8, :] = edge
    tall[:, 8 + rows2:, :] = edge
    tall[:, pl.ds(pl.multiple_of(near + 8, 8), 24), :] = u[3:11]
    near = tall[:, pl.ds(pl.multiple_of(gy * 8, 8), 24), :][:, 4:20]
    spread_rows(wide1, 0, pick(near.reshape(128, 128), spread))
    level = Level((*s1, w1), 12, False, True)
    for p in range(14):
        at = (p + 1) // 2 * 32
        start1[p] = level.u[p + 6] + wide1[0, at:at + 32, :]
    u = level.from_start(start1, 0, 14, 3, 6)

    wide = jnp.concatenate([rows_in(u, i + 3, first=4, count=24) for i in range(8)], axis=0)
    wide = pick(wide.reshape(192, 128), selector(128, 256, lambda r, c: c // 2 == r)).reshape(8, 3, 8, 256)
    level = Level((*s0, w0), 14, False, True)
    for i in range(8):
        both = jnp.concatenate([wide[i, t // 2][None] for t in range(6)], axis=0)
        start0[2 * i] = level.u[2 * i + 5] + both
        start0[2 * i + 1] = level.u[2 * i + 6] + both
    u = level.from_start(start0, 0, 16, 3, 5)

    def finish(planes):
        for i, (p, values) in enumerate(zip(planes, level.remain(u, planes, 5))):
            for which in range(2):
                for half in range(2):
                    lanes = slice(128 * half, 128 * half + 128)
                    rows_out(flat0, which, half, i, value=values[which][:, :, lanes])
                    done[which, p - 4, :, lanes] = flat0[which, half, i, 8:40]

    copies = []
    for first in (0, 4):
        finish(list(range(first + 4, first + 8)))
        for which, to in ((0, out), (1, res)):
            some = pl.ds(first, 4)
            copies.append(pltpu.make_async_copy(done.at[which, some], to.at[some], sems.at[len(copies)]))
            copies[-1].start()
    for copy in copies:
        copy.wait()


def call(body, outs, scratch, name, limit, stream=False):
    return pl.pallas_call(
        body,
        out_shape=[jax.ShapeDtypeStruct(shape, F32) for shape in outs],
        out_specs=[pl.BlockSpec(memory_space=pl.ANY if stream else pltpu.VMEM)] * len(outs),
        scratch_shapes=[
            pltpu.SemaphoreType.DMA((shape,)) if isinstance(shape, int) else pltpu.VMEM(shape, F32)
            for shape in scratch
        ],
        compiler_params=pltpu.CompilerParams(vmem_limit_bytes=limit * 1024 * 1024),
        name=name,
    )


def swap(block, axis, step, ends=0):
    count = lax.axis_size(axis)
    came = {}
    for side in (1, 0):
        pairs = [(t, t + step) for t in range(count - step) if t // step % 2 == side]
        if side and ends:
            pairs += [(0, 1), (count - 2, count - 1)]
        came[side] = lax.ppermute(block, axis, pairs + [(b, a) for a, b in pairs])
    return came[0], came[1]


def shift(block, axis, step):
    count = lax.axis_size(axis)
    return lax.ppermute(block, axis, [(t, t + step) for t in range(count) if 0 <= t + step < count])


def shards(source, conduct):
    ny = lax.axis_size("gy")

    both = jnp.stack([array[:, :, lanes] for array in (source, conduct) for lanes in (slice(0, 128), slice(128, 256))])
    both = jnp.concatenate([shift(both[:, :, 24:], "gy", 1), both, shift(both[:, :, :8], "gy", -1)], axis=2)
    first, second = swap(both, "gx", 1)
    plane = (26, 6, 8, 256)
    *s0, c1 = call(
        down0, [plane] * 7 + [(2, 8, 16, 128)], [plane] * 2 + [(4, 8, 24, 128)], "down0", 24,
    )(first, both, second)

    c1 = jnp.concatenate([shift(c1[:, :, 8:], "gy", 1), c1, shift(c1[:, :, :8], "gy", -1)], axis=2)
    first, second = swap(c1, "gx", 2, 1)
    plane = (26, 32, 128)
    *s1, c2 = call(
        down1, [plane] * 7 + [(10, 8, 128)], [plane] * 2 + [(2, 160, 128)], "down1", 12,
    )(first, c1, second)

    c2 = lax.all_to_all(jnp.broadcast_to(c2[None], (ny, 10, 8, 128)), "gy", 0, 0)
    rows = 8 * ny
    plane = (24, rows, 128)
    *s2, c3 = call(
        down2, [plane] * 7 + [(11, rows // 4, 128)], [plane] * 2 + [(1, 11 * rows, 128)], "down2", 20,
    )(shift(c2[:, 0:7], "gx", 3), c2, shift(c2[:, 3:10], "gx", -3))

    first, second = swap(c3[1:10], "gx", 6)
    out, res = call(
        upward, [(8, 32, 256)] * 2,
        [(23, rows // 2, 128)] * 9 + [(14, 24, 128)] * 2 + [(14, 32, 128)] * 2 + [(16, 6, 8, 256)] * 2
        + [(1, 7 * rows, 128), (1, 256, 128), (2, 2, 4, 48, 128), (8, 16 + rows, 128), (2, 8, 32, 256), 4],
        "upward", 32, True,
    )(first, c3, second, *s2, *s1, *s0)
    return out, res


def solution(mesh):
    spec = P("gx", "gy", None)
    return jax.shard_map(shards, mesh=mesh, in_specs=(spec, spec), out_specs=(spec, spec), check_vma=False)
```
